32 devices in a mesh: dom: 8 (over y, x, core), batch: 4 (over z).
Axes of the slice: x: 2, y: 2, z: 4, core: 2. Of those that a mesh axis runs over, the one named last changes fastest.
Arguments:
- heat_state_element: float32 [8, 8, 16, 8, 8, 128], P('dom', None, 'batch'), may hold values from -6 to 6
- wind_reference_flux: bfloat16 [3, 8, 8, 16, 8, 8, 128], P(None, 'dom', None, 'batch'), may hold values from -6 to 6
- geometric_pure_factors: bfloat16 [3, 8, 8, 16, 8, 8, 128], P(None, 'dom', None, 'batch'), may hold values from 1 to 2.5
- geometric_mixed_factors: bfloat16 [3, 8, 8, 16, 8, 8, 128], P(None, 'dom', None, 'batch'), may hold values from -0.3984375 to 0.3984375
- mapping_determinant: bfloat16 [8, 8, 16, 8, 8, 128], P('dom', None, 'batch'), may hold values from 0.5 to 2
- velocity_source_spread: float32 [8, 8, 16, 8, 8, 128], P('dom', None, 'batch'), may hold values from -1.5 to 1.5
- prior_head_state: float32 [8, 8, 16, 8, 8, 128], P('dom', None, 'batch'), may hold values from -6 to 6
- exit_boundary_marks: int32 [8, 8, 16, 8], P('dom', None, 'batch'), may hold values from 0 to 1, as said below
Outputs:
- heat_state_next: float32 [8, 8, 16, 8, 8, 128], P('dom', None, 'batch')
- head_iterate: float32 [8, 8, 16, 8, 8, 128], P('dom', None, 'batch')
- precond_residual: float32 [8, 8, 16, 8, 8, 128], P('dom', None, 'batch')
The draws below stay inside these ranges and needn't reach their ends.
Inputs may be any that keep to these rules, and one draw needn't show every extreme that they name: `exit_boundary_marks`: the flag is the same on every element copy of a shared node, the first and second directions being periodic; 1 marks an outflow node where the pressure is held at zero.
All inputs are finite; a program needn't handle non-finite values.
Results may differ from the reference program's by a relative error of at most 0.0085.
Values sent between devices are 32-bit elements; how exact they have to be, the bound alone decides.
No kernel may reach another device: no remote copies, remote signals or barrier semaphores. Data moves between devices by JAX's collectives and lax.ppermute only.
A program may use at most 128 MiB of HBM per device.

```python
import math
import jax
import jax.numpy as jnp
import numpy as np
from jax import lax

QUAD_POINT_TALLY = 8
CELLS_HEIGHTWISE = 128
ITERS = 2
CELLS_EASTWARD = 8
CELLS_NORTHWARD = 16


def draw_exit_boundary_marks(key, part):
    global_flags = jax.random.randint(key, (CELLS_EASTWARD * (QUAD_POINT_TALLY - 1), CELLS_NORTHWARD * (QUAD_POINT_TALLY - 1)), 0, 2).astype(jnp.int32)
    x_index = (jnp.arange(CELLS_EASTWARD)[:, None] * (QUAD_POINT_TALLY - 1) + jnp.arange(QUAD_POINT_TALLY)[None, :]) % (CELLS_EASTWARD * (QUAD_POINT_TALLY - 1))
    y_index = (jnp.arange(CELLS_NORTHWARD)[:, None] * (QUAD_POINT_TALLY - 1) + jnp.arange(QUAD_POINT_TALLY)[None, :]) % (CELLS_NORTHWARD * (QUAD_POINT_TALLY - 1))
    return global_flags[x_index[:, :, None, None], y_index[None, None, :, :]].astype(jnp.int32)


def steps_of(stream_key, extent, cuts, low, high):
    loudness = 1.0
    for position, blocks in cuts:
        steps = jax.random.uniform(jax.random.fold_in(jax.random.fold_in(stream_key, 6), position), (blocks,), jnp.float32, low / len(cuts), high / len(cuts))
        loudness = loudness * jnp.repeat(jnp.exp(steps), extent[position] // blocks).reshape((-1,) + (1,) * (len(extent) - 1 - position))
    return loudness


def bell_draw(stream_key, extent, scale, limit, pieces=(), dtype=jnp.bfloat16):
    entries = scale * jax.random.normal(stream_key, extent, jnp.float32)
    if pieces:
        entries = entries * steps_of(stream_key, extent, pieces, -0.22, 0.18)
    return jnp.clip(entries, -limit, limit).astype(dtype)


def setup_inputs(seed: int = 0) -> dict:
    key_of = jax.random.split(jax.random.key(seed), 9)
    return {
        "heat_state_element": bell_draw(key_of[0], (CELLS_EASTWARD, QUAD_POINT_TALLY, CELLS_NORTHWARD, QUAD_POINT_TALLY, QUAD_POINT_TALLY, CELLS_HEIGHTWISE), 1.0, 6.0, ((0, 8), (2, 4)), jnp.float32),
        "wind_reference_flux": bell_draw(key_of[1], (3, CELLS_EASTWARD, QUAD_POINT_TALLY, CELLS_NORTHWARD, QUAD_POINT_TALLY, QUAD_POINT_TALLY, CELLS_HEIGHTWISE), 1.0, 6.0, ((1, 8), (3, 4))),
        "geometric_pure_factors": jnp.clip(1.0 + 1.5 * jax.random.uniform(key_of[2], (3, CELLS_EASTWARD, QUAD_POINT_TALLY, CELLS_NORTHWARD, QUAD_POINT_TALLY, QUAD_POINT_TALLY, CELLS_HEIGHTWISE), jnp.float32) ** steps_of(key_of[2], (3, CELLS_EASTWARD, QUAD_POINT_TALLY, CELLS_NORTHWARD, QUAD_POINT_TALLY, QUAD_POINT_TALLY, CELLS_HEIGHTWISE), ((1, 8), (3, 4)), -0.2, 0.2), 1.0, 2.5).astype(jnp.bfloat16),
        "geometric_mixed_factors": jnp.clip(jax.random.uniform(key_of[3], (3, CELLS_EASTWARD, QUAD_POINT_TALLY, CELLS_NORTHWARD, QUAD_POINT_TALLY, QUAD_POINT_TALLY, CELLS_HEIGHTWISE), jnp.float32, -0.3984375, 0.3984375) * steps_of(key_of[3], (3, CELLS_EASTWARD, QUAD_POINT_TALLY, CELLS_NORTHWARD, QUAD_POINT_TALLY, QUAD_POINT_TALLY, CELLS_HEIGHTWISE), ((1, 8), (3, 4)), -0.4, 0.0), -0.3984375, 0.3984375).astype(jnp.bfloat16),
        "mapping_determinant": jnp.clip(jnp.exp(math.log(2.0) - 1.3862944 * jax.random.uniform(key_of[4], (CELLS_EASTWARD, QUAD_POINT_TALLY, CELLS_NORTHWARD, QUAD_POINT_TALLY, QUAD_POINT_TALLY, CELLS_HEIGHTWISE), jnp.float32) ** steps_of(key_of[4], (CELLS_EASTWARD, QUAD_POINT_TALLY, CELLS_NORTHWARD, QUAD_POINT_TALLY, QUAD_POINT_TALLY, CELLS_HEIGHTWISE), ((0, 8), (2, 4)), -0.2, 0.2)), 0.5, 2.0).astype(jnp.bfloat16),
        "velocity_source_spread": bell_draw(key_of[5], (CELLS_EASTWARD, QUAD_POINT_TALLY, CELLS_NORTHWARD, QUAD_POINT_TALLY, QUAD_POINT_TALLY, CELLS_HEIGHTWISE), 0.25, 1.5, ((0, 8), (2, 4)), jnp.float32),
        "prior_head_state": bell_draw(key_of[6], (CELLS_EASTWARD, QUAD_POINT_TALLY, CELLS_NORTHWARD, QUAD_POINT_TALLY, QUAD_POINT_TALLY, CELLS_HEIGHTWISE), 1.0, 6.0, ((0, 8), (2, 4)), jnp.float32),
        "exit_boundary_marks": draw_exit_boundary_marks(jax.random.fold_in(key_of[8], 71), 0),
    }


transport_increment = 0.02
conduction_increment = 0.002
step_dt = 0.02


def legendre_pair(order, point):
    before, current = 1.0, point
    for level in range(2, order + 1):
        before, current = current, ((2 * level - 1) * point * current - (level - 1) * before) / level
    return current, before


def tables():
    degree = QUAD_POINT_TALLY - 1
    points = [math.cos(math.pi * index / degree) for index in range(QUAD_POINT_TALLY)]
    for sweep in range(60):
        updated = []
        for point in points:
            top_value, below_value = legendre_pair(degree, point)
            updated.append(point - (point * top_value - below_value) / (QUAD_POINT_TALLY * top_value))
        points = updated
    gll_nodes = points[::-1]
    values = [legendre_pair(degree, point)[0] for point in gll_nodes]
    gll_weights = [2.0 / (degree * QUAD_POINT_TALLY * value * value) for value in values]
    deriv_rows = []
    for row_index in range(QUAD_POINT_TALLY):
        row_items = []
        for col_index in range(QUAD_POINT_TALLY):
            if row_index == col_index:
                row_items.append(0.0)
            else:
                row_items.append(values[row_index] / values[col_index] / (gll_nodes[row_index] - gll_nodes[col_index]))
        deriv_rows.append(row_items)
    corner_value = degree * QUAD_POINT_TALLY / 4.0
    deriv_rows[0][0] = -corner_value
    deriv_rows[QUAD_POINT_TALLY - 1][QUAD_POINT_TALLY - 1] = corner_value
    spectral_differentiator = np.array(deriv_rows)
    ends_list = [deriv_rows[index][index] for index in range(QUAD_POINT_TALLY)]
    weight_array = np.array(gll_weights)
    quad_table = weight_array[:, None, None] * weight_array[None, :, None] * weight_array[None, None, :]
    return (jnp.asarray(spectral_differentiator, jnp.float32), jnp.asarray(quad_table.reshape(1, QUAD_POINT_TALLY, 1, QUAD_POINT_TALLY, QUAD_POINT_TALLY, 1), jnp.float32), jnp.asarray(np.array(ends_list), jnp.float32))


def slope_components_out(field_in, spectral_differentiator):
    highest = lax.Precision.HIGHEST
    along_r = jnp.einsum('il,albjkz->aibjkz', spectral_differentiator, field_in, precision=highest)
    along_s = jnp.einsum('jl,aiblkz->aibjkz', spectral_differentiator, field_in, precision=highest)
    along_t = jnp.einsum('kl,aibjlz->aibjkz', spectral_differentiator, field_in, precision=highest)
    return along_r, along_s, along_t


def laplace_from(slope_component_list, geometric_pure_factors, geometric_mixed_factors, spectral_differentiator, quadrature_coefficients):
    highest = lax.Precision.HIGHEST
    along_r, along_s, along_t = slope_component_list
    diag_r = geometric_pure_factors[0].astype(jnp.float32)
    diag_s = geometric_pure_factors[1].astype(jnp.float32)
    diag_t = geometric_pure_factors[2].astype(jnp.float32)
    off_rs = geometric_mixed_factors[0].astype(jnp.float32)
    off_rt = geometric_mixed_factors[1].astype(jnp.float32)
    off_st = geometric_mixed_factors[2].astype(jnp.float32)
    flux_r = quadrature_coefficients * (diag_r * along_r + off_rs * along_s + off_rt * along_t)
    flux_s = quadrature_coefficients * (off_rs * along_r + diag_s * along_s + off_st * along_t)
    flux_t = quadrature_coefficients * (off_rt * along_r + off_st * along_s + diag_t * along_t)
    result = jnp.einsum('li,albjkz->aibjkz', spectral_differentiator, flux_r, precision=highest)
    result = result + jnp.einsum('lj,aiblkz->aibjkz', spectral_differentiator, flux_s, precision=highest)
    return result + jnp.einsum('lk,aibjlz->aibjkz', spectral_differentiator, flux_t, precision=highest)


def local_apply(field_in, geometric_pure_factors, geometric_mixed_factors, spectral_differentiator, quadrature_coefficients):
    return laplace_from(slope_components_out(field_in, spectral_differentiator), geometric_pure_factors, geometric_mixed_factors, spectral_differentiator, quadrature_coefficients)


def subdomain_source_term(heat_state_element, wind_reference_flux, geometric_pure_factors, geometric_mixed_factors, mapping_determinant, spectral_differentiator, quadrature_coefficients):
    slope_component_list = slope_components_out(heat_state_element, spectral_differentiator)
    stiffness_operator = laplace_from(slope_component_list, geometric_pure_factors, geometric_mixed_factors, spectral_differentiator, quadrature_coefficients)
    convect_scalar = wind_reference_flux[0].astype(jnp.float32) * slope_component_list[0] + wind_reference_flux[1].astype(jnp.float32) * slope_component_list[1] + wind_reference_flux[2].astype(jnp.float32) * slope_component_list[2]
    element_lumped_weights = quadrature_coefficients * mapping_determinant.astype(jnp.float32)
    return element_lumped_weights * heat_state_element - transport_increment * quadrature_coefficients * convect_scalar - conduction_increment * stiffness_operator


def jacobi_diagonal(geometric_pure_factors, geometric_mixed_factors, spectral_differentiator, quadrature_coefficients, deriv_ends):
    highest = lax.Precision.HIGHEST
    squares = spectral_differentiator * spectral_differentiator
    result = jnp.einsum('li,albjkz->aibjkz', squares, quadrature_coefficients * geometric_pure_factors[0].astype(jnp.float32), precision=highest)
    result = result + jnp.einsum('lj,aiblkz->aibjkz', squares, quadrature_coefficients * geometric_pure_factors[1].astype(jnp.float32), precision=highest)
    result = result + jnp.einsum('lk,aibjlz->aibjkz', squares, quadrature_coefficients * geometric_pure_factors[2].astype(jnp.float32), precision=highest)
    end_i = deriv_ends.reshape(1, QUAD_POINT_TALLY, 1, 1, 1, 1)
    end_j = deriv_ends.reshape(1, 1, 1, QUAD_POINT_TALLY, 1, 1)
    end_k = deriv_ends.reshape(1, 1, 1, 1, QUAD_POINT_TALLY, 1)
    cross = geometric_mixed_factors[0].astype(jnp.float32) * end_i * end_j + geometric_mixed_factors[1].astype(jnp.float32) * end_i * end_k + geometric_mixed_factors[2].astype(jnp.float32) * end_j * end_k
    return result + 2.0 * quadrature_coefficients * cross


def vertical_sums(node_grid):
    upper = node_grid[..., QUAD_POINT_TALLY - 1, :]
    lower = node_grid[..., 0, :]
    joined = upper[..., :-1] + lower[..., 1:]
    new_upper = jnp.concatenate([joined, upper[..., -1:]], axis=-1)
    new_lower = jnp.concatenate([lower[..., :1], joined], axis=-1)
    return jnp.concatenate([new_lower[..., None, :], node_grid[..., 1:QUAD_POINT_TALLY - 1, :], new_upper[..., None, :]], axis=-2)


def node_weights(vertical_layer_tally):
    points = jnp.arange(QUAD_POINT_TALLY)
    layers = jnp.arange(vertical_layer_tally)
    edge_copies = jnp.where((points == 0) | (points == QUAD_POINT_TALLY - 1), 2.0, 1.0).astype(jnp.float32)
    vertical = jnp.where(((points[:, None] == 0) & (layers[None, :] > 0)) | ((points[:, None] == QUAD_POINT_TALLY - 1) & (layers[None, :] < vertical_layer_tally - 1)), 2.0, 1.0).astype(jnp.float32)
    copies = edge_copies.reshape(1, QUAD_POINT_TALLY, 1, 1, 1, 1) * edge_copies.reshape(1, 1, 1, QUAD_POINT_TALLY, 1, 1) * vertical.reshape(1, 1, 1, 1, QUAD_POINT_TALLY, vertical_layer_tally)
    return (1.0 / copies).astype(jnp.float32)


def keep_mask(exit_boundary_marks, vertical_layer_tally):
    points = jnp.arange(QUAD_POINT_TALLY)
    layers = jnp.arange(vertical_layer_tally)
    top_face = ((points[:, None] == QUAD_POINT_TALLY - 1) & (layers[None, :] == vertical_layer_tally - 1)).astype(jnp.float32)
    return 1.0 - exit_boundary_marks.astype(jnp.float32)[:, :, :, :, None, None] * top_face


def assemble_shared_nodal(field_in):
    field_in = vertical_sums(field_in)
    joined = field_in[:, QUAD_POINT_TALLY - 1] + jnp.roll(field_in[:, 0], -1, axis=0)
    field_in = field_in.at[:, QUAD_POINT_TALLY - 1].set(joined).at[:, 0].set(jnp.roll(joined, 1, axis=0))
    joined = field_in[:, :, :, QUAD_POINT_TALLY - 1] + jnp.roll(field_in[:, :, :, 0], -1, axis=2)
    return field_in.at[:, :, :, QUAD_POINT_TALLY - 1].set(joined).at[:, :, :, 0].set(jnp.roll(joined, 1, axis=2))


def reference(heat_state_element, wind_reference_flux, geometric_pure_factors, geometric_mixed_factors, mapping_determinant, velocity_source_spread, prior_head_state, exit_boundary_marks):
    spectral_differentiator, quadrature_coefficients, deriv_ends = tables()
    wind_flux_moved = jnp.moveaxis(wind_reference_flux, 1, 0)
    pure_factors_moved = jnp.moveaxis(geometric_pure_factors, 1, 0)
    mixed_factors_moved = jnp.moveaxis(geometric_mixed_factors, 1, 0)

    def subdomain_element_block(items):
        temp_slab, vel_slab, diag_slab, off_slab, jac_slab = items
        numer = subdomain_source_term(temp_slab[None], vel_slab[:, None], diag_slab[:, None], off_slab[:, None], jac_slab[None], spectral_differentiator, quadrature_coefficients)
        jdiag = jacobi_diagonal(diag_slab[:, None], off_slab[:, None], spectral_differentiator, quadrature_coefficients, deriv_ends)
        return numer[0], jdiag[0]

    def apply_slab(items):
        field_slab, diag_slab, off_slab = items
        return local_apply(field_slab[None], diag_slab[:, None], off_slab[:, None], spectral_differentiator, quadrature_coefficients)[0]

    def apply_all(field_in):
        return lax.map(apply_slab, (field_in, pure_factors_moved, mixed_factors_moved))

    quotient_top_part, element_main_entries = lax.map(subdomain_element_block, (heat_state_element, wind_flux_moved, pure_factors_moved, mixed_factors_moved, mapping_determinant))
    element_lumped_weights = quadrature_coefficients * mapping_determinant.astype(jnp.float32)
    assembled_lumped_weights = assemble_shared_nodal(element_lumped_weights)
    heat_state_next = assemble_shared_nodal(quotient_top_part) / assembled_lumped_weights
    vertical_layer_tally = heat_state_element.shape[-1]
    keep_nodes = keep_mask(exit_boundary_marks, vertical_layer_tally)
    weights = node_weights(vertical_layer_tally)
    jacobi_diag = assemble_shared_nodal(element_main_entries)
    head_iterate = keep_nodes * assemble_shared_nodal(element_lumped_weights * prior_head_state) / assembled_lumped_weights
    source_local = -element_lumped_weights * velocity_source_spread / step_dt
    residual = keep_nodes * assemble_shared_nodal(source_local - apply_all(head_iterate))
    preconditioned_defect = residual / jacobi_diag
    precond_dot = jnp.sum(residual * preconditioned_defect * weights)
    direction = preconditioned_defect
    for iteration in range(ITERS):
        image_vec = keep_nodes * assemble_shared_nodal(apply_all(direction))
        step_size = precond_dot / jnp.sum(direction * image_vec * weights)
        head_iterate = head_iterate + step_size * direction
        residual = residual - step_size * image_vec
        preconditioned_defect = residual / jacobi_diag
        if iteration + 1 < ITERS:
            dot_next = jnp.sum(residual * preconditioned_defect * weights)
            direction = preconditioned_defect + (dot_next / precond_dot) * direction
            precond_dot = dot_next
    return heat_state_next, head_iterate, preconditioned_defect
```

```python
import functools
import math

import jax
import jax.numpy as jnp
import numpy as np
from jax import lax
from jax.experimental import pallas as pl
from jax.experimental.pallas import tpu as pltpu
from jax.sharding import PartitionSpec as P

QUAD_POINT_TALLY = 8
ROWS = QUAD_POINT_TALLY * QUAD_POINT_TALLY
LAST = ROWS - QUAD_POINT_TALLY
ITERS = 2

transport_increment = 0.02
conduction_increment = 0.002
step_dt = 0.02

VMEM_LIMIT = 24 * 1024 * 1024


def legendre_pair(order, point):
    before, current = (1.0, point)
    for level in range(2, order + 1):
        before, current = (
            current,
            ((2 * level - 1) * point * current - (level - 1) * before) / level,
        )
    return (current, before)


def tables():
    degree = QUAD_POINT_TALLY - 1
    points = [math.cos(math.pi * index / degree) for index in range(QUAD_POINT_TALLY)]
    for sweep in range(60):
        updated = []
        for point in points:
            top_value, below_value = legendre_pair(degree, point)
            updated.append(
                point - (point * top_value - below_value) / (QUAD_POINT_TALLY * top_value)
            )
        points = updated
    nodes = points[::-1]
    values = [legendre_pair(degree, point)[0] for point in nodes]
    weights = [2.0 / (degree * QUAD_POINT_TALLY * value * value) for value in values]
    deriv = np.zeros((QUAD_POINT_TALLY, QUAD_POINT_TALLY))
    for row in range(QUAD_POINT_TALLY):
        for col in range(QUAD_POINT_TALLY):
            if row != col:
                deriv[row, col] = values[row] / values[col] / (nodes[row] - nodes[col])
    corner_value = degree * QUAD_POINT_TALLY / 4.0
    deriv[0, 0] = -corner_value
    deriv[degree, degree] = corner_value
    return deriv, np.array(weights)


DERIV, WEIGHTS = tables()
HALF = QUAD_POINT_TALLY // 2


def line_tables(matrix):
    flipped = matrix[:, ::-1]
    even = (matrix + flipped)[:HALF, :HALF] / 2
    odd = (matrix - flipped)[:HALF, :HALF] / 2
    return even, odd


def line_product(matrix, values, sign):
    even, odd = line_tables(matrix)
    plus = [values[l] + values[7 - l] for l in range(HALF)]
    minus = [values[l] - values[7 - l] for l in range(HALF)]
    result = [None] * QUAD_POINT_TALLY
    for i in range(HALF):
        from_plus = sum(float(even[i, l]) * plus[l] for l in range(HALF))
        from_minus = sum(float(odd[i, l]) * minus[l] for l in range(HALF))
        result[i] = from_plus + from_minus
        flip = from_plus - from_minus
        result[7 - i] = flip if sign > 0 else -flip
    return result


def deriv_line(matrix, values):
    even, odd = line_tables(matrix)
    plus = [values[l] + values[7 - l] for l in range(HALF)]
    minus = [values[l] - values[7 - l] for l in range(HALF)]
    result = [None] * QUAD_POINT_TALLY
    for i in range(HALF):
        from_plus = sum(float(even[i, l]) * plus[l] for l in range(HALF))
        from_minus = sum(float(odd[i, l]) * minus[l] for l in range(HALF))
        result[i] = from_minus + from_plus
        result[7 - i] = from_minus - from_plus
    return result


def square_line(matrix, values):
    even, odd = line_tables(matrix)
    plus = [values[l] + values[7 - l] for l in range(HALF)]
    minus = [values[l] - values[7 - l] for l in range(HALF)]
    result = [None] * QUAD_POINT_TALLY
    for i in range(HALF):
        from_plus = sum(float(even[i, l]) * plus[l] for l in range(HALF))
        from_minus = sum(float(odd[i, l]) * minus[l] for l in range(HALF))
        result[i] = from_plus + from_minus
        result[7 - i] = from_plus - from_minus
    return result


def stacked_matrix(matrix):
    whole = np.kron(np.eye(QUAD_POINT_TALLY), matrix).astype(np.float32)
    high = whole.astype(jnp.bfloat16)
    low = (whole - high.astype(np.float32)).astype(jnp.bfloat16)
    return np.concatenate([high, low, high], axis=1)


def height_product(stacked, values):
    high = values.astype(jnp.bfloat16)
    low = (values - high.astype(jnp.float32)).astype(jnp.bfloat16)
    both = jnp.concatenate([high, high, low], axis=0)
    return jnp.dot(stacked, both, preferred_element_type=jnp.float32)


def rows_of(j):
    return slice(QUAD_POINT_TALLY * j, QUAD_POINT_TALLY * (j + 1))


def height_weights(shape):
    level = lax.broadcasted_iota(jnp.int32, shape, 0)
    result = jnp.full(shape, float(WEIGHTS[0]), jnp.float32)
    for k in range(1, QUAD_POINT_TALLY):
        result = jnp.where(level == k, float(WEIGHTS[k]), result)
    return result


def copy_weights(shape):
    level = lax.broadcasted_iota(jnp.int32, shape, 0)
    layer = lax.broadcasted_iota(jnp.int32, shape, 1)
    shared = ((level == 0) & (layer > 0)) | (
        (level == QUAD_POINT_TALLY - 1) & (layer < shape[1] - 1)
    )
    return jnp.where(shared, 0.5, 1.0)


def side_weight(i, j):
    return (0.5 if i in (0, 7) else 1.0) * (0.5 if j in (0, 7) else 1.0)


def dom_sides():
    odd = lax.rem(lax.axis_index("dom"), 2)
    return 7 * (1 - odd), 7 * odd


def batch_sides():
    odd = lax.rem(lax.axis_index("batch"), 2)
    return 1 - odd, odd


def sum_within(field):
    blocks, layers = field.shape[1], field.shape[3]
    lane = lax.broadcasted_iota(jnp.int32, (QUAD_POINT_TALLY, layers), 1)
    upper_rows = pl.ds(QUAD_POINT_TALLY - 1, QUAD_POINT_TALLY, stride=QUAD_POINT_TALLY)
    lower_rows = pl.ds(0, QUAD_POINT_TALLY, stride=QUAD_POINT_TALLY)
    for i in range(QUAD_POINT_TALLY):
        for b in range(blocks):
            upper = field[i, b, upper_rows, :]
            lower = field[i, b, lower_rows, :]
            above = jnp.where(lane < layers - 1, pltpu.roll(lower, layers - 1, 1), 0.0)
            below = jnp.where(lane > 0, pltpu.roll(upper, 1, 1), 0.0)
            field[i, b, upper_rows, :] = upper + above
            field[i, b, lower_rows, :] = lower + below
        for b in range(blocks - 1):
            joined = field[i, b, LAST:ROWS, :] + field[i, b + 1, 0:QUAD_POINT_TALLY, :]
            field[i, b, LAST:ROWS, :] = joined
            field[i, b + 1, 0:QUAD_POINT_TALLY, :] = joined


def emit_faces(field, first, second, ends):
    blocks = field.shape[1]
    side_first, side_second = dom_sides()
    for b in range(blocks):
        first[b] = field[side_first, b]
        second[b] = field[side_second, b]
    for i in range(QUAD_POINT_TALLY):
        ends[0, i] = field[i, 0, 0:QUAD_POINT_TALLY, :]
        ends[1, i] = field[i, blocks - 1, LAST:ROWS, :]


def add_received(field, dom_first, dom_second, batch_first, batch_second):
    blocks = field.shape[1]
    side_first, side_second = dom_sides()
    for b in range(blocks):
        field[side_first, b] = field[side_first, b] + dom_first[b]
        field[side_second, b] = field[side_second, b] + dom_second[b]
    for side, received in zip(batch_sides(), (batch_first, batch_second)):
        block = side * (blocks - 1)
        rows = pl.ds(pl.multiple_of(side * LAST, QUAD_POINT_TALLY), QUAD_POINT_TALLY)
        for i in range(QUAD_POINT_TALLY):
            field[i, block, rows, :] = field[i, block, rows, :] + received[i]


def clear_top(field, keep):
    upper_rows = pl.ds(QUAD_POINT_TALLY - 1, QUAD_POINT_TALLY, stride=QUAD_POINT_TALLY)
    for i in range(QUAD_POINT_TALLY):
        for b in range(field.shape[1]):
            field[i, b, upper_rows, :] = field[i, b, upper_rows, :] * keep[i, b]


def apply_block(field, metric, scratch_s, scratch_t, out, b, scale, height, height_back, extra=None):
    back = scale * DERIV.T
    for i in range(QUAD_POINT_TALLY):
        block = field[i, b]
        along_s = deriv_line(DERIV, [block[rows_of(j)] for j in range(QUAD_POINT_TALLY)])
        for j in range(QUAD_POINT_TALLY):
            scratch_s[i, rows_of(j), :] = along_s[j]
        scratch_t[i] = height_product(height, block)
    for j in range(QUAD_POINT_TALLY):
        rows = rows_of(j)
        along_r = deriv_line(DERIV, [field[i, b, rows, :] for i in range(QUAD_POINT_TALLY)])
        flux_r = []
        additions = []
        for i in range(QUAD_POINT_TALLY):
            along_s, along_t = scratch_s[i, rows, :], scratch_t[i, rows, :]
            rr, ss, tt = (metric[n, i, b, rows, :] for n in range(3))
            rs, rt, st = (metric[n, i, b, rows, :] for n in range(3, 6))
            flux_r.append(rr * along_r[i] + rs * along_s + rt * along_t)
            scratch_s[i, rows, :] = rs * along_r[i] + ss * along_s + st * along_t
            scratch_t[i, rows, :] = rt * along_r[i] + st * along_s + tt * along_t
            if extra is not None:
                additions.append(extra(i, j, along_r[i], along_s, along_t))
        result = deriv_line(back, flux_r)
        for i in range(QUAD_POINT_TALLY):
            out[i, b, rows, :] = result[i] if extra is None else result[i] + additions[i]
    total = None
    for i in range(QUAD_POINT_TALLY):
        block = scratch_s[i]
        from_s = deriv_line(back, [block[rows_of(j)] for j in range(QUAD_POINT_TALLY)])
        from_t = height_product(height_back, scratch_t[i])
        for j in range(QUAD_POINT_TALLY):
            rows = rows_of(j)
            value = out[i, b, rows, :] + from_s[j] + from_t[rows]
            out[i, b, rows, :] = value
            if extra is None:
                term = field[i, b, rows, :] * value
                total = term if total is None else total + term
    return total


def dot_weighted(left, right):
    blocks, layers = left.shape[1], left.shape[3]
    sums = {}
    for i in range(QUAD_POINT_TALLY):
        for b in range(blocks):
            for j in range(QUAD_POINT_TALLY):
                weight = side_weight(i, j)
                term = left[i, b, rows_of(j), :] * right[i, b, rows_of(j), :]
                sums[weight] = sums[weight] + term if weight in sums else term
    total = sums[1.0] + 0.5 * sums[0.5] + 0.25 * sums[0.25]
    return total * copy_weights((QUAD_POINT_TALLY, layers))


def mass_kernel(determinant, prior, mass, mass_prior, first, second, ends):
    blocks, layers = mass.shape[1], mass.shape[3]
    weights = height_weights((QUAD_POINT_TALLY, layers))

    def block(b, carry):
        for i in range(QUAD_POINT_TALLY):
            for j in range(QUAD_POINT_TALLY):
                weight = weights * float(WEIGHTS[i] * WEIGHTS[j])
                value = weight * determinant[i, b, j].astype(jnp.float32)
                mass[i, b, rows_of(j), :] = value
                mass_prior[i, b, rows_of(j), :] = value * prior[i, b, rows_of(j), :]
        return carry

    lax.fori_loop(0, blocks, block, 0)
    for n, field in enumerate((mass, mass_prior)):
        sum_within(field)
        emit_faces(field, first.at[n], second.at[n], ends.at[n])


def metric_kernel(pure, mixed, height_square, metric, diagonal):
    blocks, layers = diagonal.shape[1], diagonal.shape[3]
    weights = height_weights((QUAD_POINT_TALLY, layers))
    level = lax.broadcasted_iota(jnp.int32, (QUAD_POINT_TALLY, layers), 0)
    ends = [float(DERIV[i, i]) for i in range(QUAD_POINT_TALLY)]
    height_ends = jnp.where(level == 0, ends[0], jnp.where(level == 7, ends[7], 0.0))
    squares = DERIV * DERIV

    def block(b, carry):
        for i in range(QUAD_POINT_TALLY):
            for j in range(QUAD_POINT_TALLY):
                weight = weights * float(WEIGHTS[i] * WEIGHTS[j])
                for n in range(3):
                    metric[n, i, b, rows_of(j), :] = weight * pure[n, i, b, j].astype(jnp.float32)
                    metric[n + 3, i, b, rows_of(j), :] = weight * mixed[n, i, b, j].astype(
                        jnp.float32
                    )
        for j in range(QUAD_POINT_TALLY):
            line = square_line(
                squares.T, [metric[0, i, b, rows_of(j), :] for i in range(QUAD_POINT_TALLY)]
            )
            for i in range(QUAD_POINT_TALLY):
                diagonal[i, b, rows_of(j), :] = line[i]
        for i in range(QUAD_POINT_TALLY):
            line = square_line(
                squares.T, [metric[1, i, b, rows_of(j), :] for j in range(QUAD_POINT_TALLY)]
            )
            from_t = height_product(height_square[...], metric[2, i, b])
            for j in range(QUAD_POINT_TALLY):
                rows = rows_of(j)
                value = diagonal[i, b, rows, :] + line[j] + from_t[rows]
                if ends[i] != 0.0 and ends[j] != 0.0:
                    value = value + (2.0 * ends[i] * ends[j]) * metric[3, i, b, rows, :]
                if ends[i] != 0.0:
                    value = value + (2.0 * ends[i]) * height_ends * metric[4, i, b, rows, :]
                if ends[j] != 0.0:
                    value = value + (2.0 * ends[j]) * height_ends * metric[5, i, b, rows, :]
                diagonal[i, b, rows, :] = value
        return carry

    lax.fori_loop(0, blocks, block, 0)
    sum_within(diagonal)


def source_kernel(
    metric, heat, wind, determinant, diagonal, height, height_back,
    numerator, first, second, ends, scratch_s, scratch_t,
):
    blocks, layers = numerator.shape[1], numerator.shape[3]
    weights = height_weights((QUAD_POINT_TALLY, layers))

    def block(b, carry):
        def extra(i, j, along_r, along_s, along_t):
            weight = weights * float(WEIGHTS[i] * WEIGHTS[j])
            convection = (
                wind[0, i, b, j].astype(jnp.float32) * along_r
                + wind[1, i, b, j].astype(jnp.float32) * along_s
                + wind[2, i, b, j].astype(jnp.float32) * along_t
            )
            return weight * (
                determinant[i, b, j].astype(jnp.float32) * heat[i, b, rows_of(j), :]
                - transport_increment * convection
            )

        apply_block(
            heat, metric, scratch_s, scratch_t, numerator, b, -conduction_increment,
            height[...], height_back[...], extra,
        )
        return carry

    lax.fori_loop(0, blocks, block, 0)
    sum_within(numerator)
    for n, field in enumerate((diagonal, numerator)):
        emit_faces(field, first.at[n], second.at[n], ends.at[n])


def ends_kernel(groups, *refs):
    inputs, (first, second) = refs[: 3 * groups], refs[3 * groups :]
    side_first, side_second = dom_sides()
    base = 0
    for group in range(groups):
        ends, dom_first, dom_second = inputs[3 * group : 3 * group + 3]
        blocks = dom_first.shape[1]
        for n in range(ends.shape[0]):
            for side, target in zip(batch_sides(), (first, second)):
                block = side * (blocks - 1)
                rows = pl.ds(pl.multiple_of(side * LAST, QUAD_POINT_TALLY), QUAD_POINT_TALLY)
                for i in range(QUAD_POINT_TALLY):
                    target[base + n, i] = ends[n, side, i]
                for dom_side, received in (
                    (side_first, dom_first),
                    (side_second, dom_second),
                ):
                    target[base + n, dom_side] = (
                        target[base + n, dom_side] + received[n, block, rows, :]
                    )
        base += ends.shape[0]


def start_kernel(
    mass_local, prior_local, dom_first, dom_second, batch_first, batch_second,
    metric, spread, determinant, keep, height, height_back,
    head, mass_inverse, residual, first, second, ends, scratch_s, scratch_t,
):
    blocks, layers = head.shape[1], head.shape[3]
    weights = height_weights((QUAD_POINT_TALLY, layers))
    head[...] = prior_local[...]
    mass_inverse[...] = mass_local[...]
    for n, field in enumerate((mass_inverse, head)):
        add_received(
            field, dom_first.at[n], dom_second.at[n], batch_first.at[n], batch_second.at[n]
        )
    clear_top(head, keep)

    def divide(b, carry):
        for i in range(QUAD_POINT_TALLY):
            inverse = 1.0 / mass_inverse[i, b]
            mass_inverse[i, b] = inverse
            head[i, b] = head[i, b] * inverse
        return carry

    lax.fori_loop(0, blocks, divide, 0)

    def block(b, carry):
        def extra(i, j, along_r, along_s, along_t):
            weight = weights * float(WEIGHTS[i] * WEIGHTS[j] / step_dt)
            return -(weight * determinant[i, b, j].astype(jnp.float32)) * spread[i, b, rows_of(j), :]

        apply_block(
            head, metric, scratch_s, scratch_t, residual, b, -1.0,
            height[...], height_back[...], extra,
        )
        return carry

    lax.fori_loop(0, blocks, block, 0)
    sum_within(residual)
    emit_faces(residual, first.at[0], second.at[0], ends.at[0])


def apply_all(field, metric, scratch_s, scratch_t, out, height, height_back):
    blocks, layers = field.shape[1], field.shape[3]

    def block(b, total):
        return total + apply_block(
            field, metric, scratch_s, scratch_t, out, b, 1.0, height[...], height_back[...]
        )

    return lax.fori_loop(
        0, blocks, block, jnp.zeros((QUAD_POINT_TALLY, layers), jnp.float32)
    )


def first_kernel(
    residual_local, diagonal_local, res_first, res_second, diag_first, diag_second,
    batch_first, batch_second, metric, keep, height, height_back,
    direction, diag_inverse, image, first, second, ends, dots, scratch_s, scratch_t, residual,
):
    blocks = direction.shape[1]
    residual[...] = residual_local[...]
    diag_inverse[...] = diagonal_local[...]
    add_received(residual, res_first.at[0], res_second.at[0], batch_first.at[0], batch_second.at[0])
    add_received(
        diag_inverse, diag_first.at[0], diag_second.at[0], batch_first.at[1], batch_second.at[1]
    )
    clear_top(residual, keep)

    def divide(b, carry):
        for i in range(QUAD_POINT_TALLY):
            inverse = 1.0 / diag_inverse[i, b]
            diag_inverse[i, b] = inverse
            direction[i, b] = residual[i, b] * inverse
        return carry

    lax.fori_loop(0, blocks, divide, 0)
    inner = dot_weighted(residual, direction)
    energy = apply_all(direction, metric, scratch_s, scratch_t, image, height, height_back)
    sum_within(image)
    emit_faces(image, first.at[0], second.at[0], ends.at[0])
    dots[...] = jnp.concatenate(
        [jnp.sum(inner, axis=0, keepdims=True), jnp.sum(energy, axis=0, keepdims=True),
         jnp.zeros((6, inner.shape[1]), jnp.float32)], axis=0,
    )


def second_kernel(
    image_local, dom_first, dom_second, batch_first, batch_second,
    diag_inverse, metric, keep, dots, height, height_back,
    scaled, image_two, first, second, ends, all_dots, scratch_s, scratch_t, image,
):
    blocks = scaled.shape[1]
    image[...] = image_local[...]
    add_received(image, dom_first.at[0], dom_second.at[0], batch_first.at[0], batch_second.at[0])
    clear_top(image, keep)

    def divide(b, carry):
        for i in range(QUAD_POINT_TALLY):
            scaled[i, b] = image[i, b] * diag_inverse[i, b]
        return carry

    lax.fori_loop(0, blocks, divide, 0)
    inner = dot_weighted(image, scaled)
    energy = apply_all(scaled, metric, scratch_s, scratch_t, image_two, height, height_back)
    sum_within(image_two)
    emit_faces(image_two, first.at[0], second.at[0], ends.at[0])
    total = jnp.concatenate(
        [dots[0:2], jnp.sum(inner, axis=0, keepdims=True), jnp.sum(energy, axis=0, keepdims=True),
         dots[4:8]], axis=0,
    )
    for n in range(all_dots.shape[0]):
        all_dots[n] = total


def heat_kernel(
    numerator, dom_first, dom_second, batch_first, batch_second, mass_inverse, heat
):
    heat[...] = numerator[...]
    add_received(heat, dom_first.at[1], dom_second.at[1], batch_first.at[2], batch_second.at[2])
    for b in range(heat.shape[1]):
        for i in range(QUAD_POINT_TALLY):
            heat[i, b] = heat[i, b] * mass_inverse[i, b]


def last_kernel(
    image_local, dom_first, dom_second, batch_first, batch_second,
    diag_inverse, head, direction, scaled, keep, all_dots, out_head, out_defect, image,
):
    blocks = head.shape[1]
    image[...] = image_local[...]
    add_received(image, dom_first.at[0], dom_second.at[0], batch_first.at[0], batch_second.at[0])
    clear_top(image, keep)
    sums = all_dots[0]
    for n in range(1, all_dots.shape[0]):
        sums = sums + all_dots[n]
    sums = jnp.sum(sums, axis=1, keepdims=True)
    inner, energy, cross, energy_two = (sums[n : n + 1] for n in range(4))
    step = inner / energy
    following = step * step * cross - inner
    growth = 1.0 + following / inner
    curvature = growth * growth * energy - 2.0 * growth * step * cross + step * step * energy_two
    step_two = following / curvature
    along_direction = step + step_two * growth
    along_scaled = step * step_two

    def block(b, carry):
        for i in range(QUAD_POINT_TALLY):
            start, change = direction[i, b], scaled[i, b]
            second_change = image[i, b] * diag_inverse[i, b]
            out_head[i, b] = head[i, b] + along_direction * start - along_scaled * change
            out_defect[i, b] = start - along_direction * change + along_scaled * second_change
        return carry

    lax.fori_loop(0, blocks, block, 0)


def call(kernel, name, outs, args, scratch=()):
    whole = pl.BlockSpec(memory_space=pltpu.VMEM)
    return pl.pallas_call(
        kernel,
        name=name,
        out_shape=[jax.ShapeDtypeStruct(shape, jnp.float32) for shape in outs],
        in_specs=[whole] * len(args),
        out_specs=[whole] * len(outs),
        scratch_shapes=[pltpu.VMEM(shape, jnp.float32) for shape in scratch],
        compiler_params=pltpu.CompilerParams(vmem_limit_bytes=VMEM_LIMIT),
    )(*args)


def swaps(first, second, axis):
    count = lax.axis_size(axis)
    near = [(index, index ^ 1) for index in range(count)]
    far = [(index, (((index + 1) ^ 1) - 1) % count) for index in range(count)]
    return lax.ppermute(first, axis, near), lax.ppermute(second, axis, far)


def shards(
    heat_state_element,
    wind_reference_flux,
    geometric_pure_factors,
    geometric_mixed_factors,
    mapping_determinant,
    velocity_source_spread,
    prior_head_state,
    exit_boundary_marks,
):
    _, points, blocks, _, _, layers = heat_state_element.shape
    block_shape = (points, blocks, ROWS, layers)
    heat = heat_state_element.reshape(block_shape)
    spread = velocity_source_spread.reshape(block_shape)
    prior = prior_head_state.reshape(block_shape)
    wind, pure, mixed = (
        array.reshape(array.shape[:1] + array.shape[2:])
        for array in (wind_reference_flux, geometric_pure_factors, geometric_mixed_factors)
    )
    determinant = mapping_determinant[0]
    layer = lax.broadcasted_iota(jnp.int32, (points, blocks, points, layers), 3)
    marks = exit_boundary_marks[0].astype(jnp.float32)[:, :, :, None]
    keep = jnp.where(layer == layers - 1, 1.0 - marks, 1.0)

    height = jnp.asarray(stacked_matrix(DERIV))
    height_back = jnp.asarray(stacked_matrix(DERIV.T))
    height_back_minus = jnp.asarray(stacked_matrix(-DERIV.T))
    height_back_heat = jnp.asarray(stacked_matrix(-conduction_increment * DERIV.T))
    height_square = jnp.asarray(stacked_matrix((DERIV * DERIV).T))

    def faces(count):
        return [(count, blocks, ROWS, layers)] * 2 + [(count, 2, points, points, layers)]

    def ends_call(name, *groups):
        count = sum(group[0].shape[0] for group in groups)
        return call(
            functools.partial(ends_kernel, len(groups)),
            name,
            [(count, points, points, layers)] * 2,
            [array for group in groups for array in group],
        )

    pair = [(points, ROWS, layers)] * 2

    mass, mass_prior, *mass_faces, mass_ends = call(
        mass_kernel, "mass", [block_shape] * 2 + faces(2), [determinant, prior]
    )
    mass_dom = swaps(*mass_faces, "dom")
    metric, diagonal = call(
        metric_kernel, "metric", [(6,) + block_shape, block_shape], [pure, mixed, height_square]
    )
    numerator, *source_faces, source_ends = call(
        source_kernel, "source", [block_shape] + faces(2),
        [metric, heat, wind, determinant, diagonal, height, height_back_heat], pair,
    )
    source_dom = swaps(*source_faces, "dom")
    mass_batch = swaps(*ends_call("mass_ends", (mass_ends, *mass_dom)), "batch")
    head, mass_inverse, residual, *res_faces, res_ends = call(
        start_kernel, "start", [block_shape] * 3 + faces(1),
        [mass, mass_prior, *mass_dom, *mass_batch, metric, spread, determinant, keep,
         height, height_back_minus], pair,
    )
    res_dom = swaps(*res_faces, "dom")
    res_batch = swaps(
        *ends_call("res_ends", (res_ends, *res_dom), (source_ends, *source_dom)), "batch"
    )
    direction, diag_inverse, image, *image_faces, image_ends, dots = call(
        first_kernel, "first", [block_shape] * 3 + faces(1) + [(points, layers)],
        [residual, diagonal, *res_dom, *source_dom, *res_batch, metric, keep,
         height, height_back], pair + [block_shape],
    )
    image_dom = swaps(*image_faces, "dom")
    image_batch = swaps(*ends_call("image_ends", (image_ends, *image_dom)), "batch")
    count = lax.axis_size("dom") * lax.axis_size("batch")
    scaled, image_two, *two_faces, two_ends, all_dots = call(
        second_kernel, "second",
        [block_shape] * 2 + faces(1) + [(count, points, layers)],
        [image, *image_dom, *image_batch, diag_inverse, metric, keep, dots, height, height_back],
        pair + [block_shape],
    )
    two_dom = swaps(*two_faces, "dom")
    all_dots = lax.all_to_all(all_dots, ("dom", "batch"), 0, 0)
    two_batch = swaps(*ends_call("two_ends", (two_ends, *two_dom)), "batch")
    heat_next, = call(
        heat_kernel, "heat", [block_shape],
        [numerator, *source_dom, *res_batch, mass_inverse],
    )
    head_next, defect = call(
        last_kernel, "last", [block_shape] * 2,
        [image_two, *two_dom, *two_batch, diag_inverse, head, direction, scaled, keep, all_dots],
        [block_shape],
    )
    shape = heat_state_element.shape
    return heat_next.reshape(shape), head_next.reshape(shape), defect.reshape(shape)


def solution(mesh):
    field = P("dom", None, "batch", None, None, None)
    triple = P(None, "dom", None, "batch", None, None, None)
    return jax.shard_map(
        shards,
        mesh=mesh,
        in_specs=(
            field, triple, triple, triple, field, field, field, P("dom", None, "batch", None),
        ),
        out_specs=(field, field, field),
        check_vma=False,
    )
```

```python
import functools
import math

import jax
import jax.numpy as jnp
import numpy as np
from jax import lax
from jax.experimental import pallas as pl
from jax.experimental.pallas import tpu as pltpu
from jax.sharding import PartitionSpec as P

QUAD_POINT_TALLY = 8
ROWS = QUAD_POINT_TALLY * QUAD_POINT_TALLY
LAST = ROWS - QUAD_POINT_TALLY
ITERS = 2

transport_increment = 0.02
conduction_increment = 0.002
step_dt = 0.02

VMEM_LIMIT = 12 * 1024 * 1024


def legendre_pair(order, point):
    before, current = (1.0, point)
    for level in range(2, order + 1):
        before, current = (
            current,
            ((2 * level - 1) * point * current - (level - 1) * before) / level,
        )
    return (current, before)


def tables():
    degree = QUAD_POINT_TALLY - 1
    points = [math.cos(math.pi * index / degree) for index in range(QUAD_POINT_TALLY)]
    for sweep in range(60):
        updated = []
        for point in points:
            top_value, below_value = legendre_pair(degree, point)
            updated.append(
                point - (point * top_value - below_value) / (QUAD_POINT_TALLY * top_value)
            )
        points = updated
    nodes = points[::-1]
    values = [legendre_pair(degree, point)[0] for point in nodes]
    weights = [2.0 / (degree * QUAD_POINT_TALLY * value * value) for value in values]
    deriv = np.zeros((QUAD_POINT_TALLY, QUAD_POINT_TALLY))
    for row in range(QUAD_POINT_TALLY):
        for col in range(QUAD_POINT_TALLY):
            if row != col:
                deriv[row, col] = values[row] / values[col] / (nodes[row] - nodes[col])
    corner_value = degree * QUAD_POINT_TALLY / 4.0
    deriv[0, 0] = -corner_value
    deriv[degree, degree] = corner_value
    return deriv, np.array(weights)


DERIV, WEIGHTS = tables()
HALF = QUAD_POINT_TALLY // 2


def line_tables(matrix):
    flipped = matrix[:, ::-1]
    even = (matrix + flipped)[:HALF, :HALF] / 2
    odd = (matrix - flipped)[:HALF, :HALF] / 2
    return even, odd


def deriv_line(matrix, values):
    even, odd = line_tables(matrix)
    plus = [values[l] + values[7 - l] for l in range(HALF)]
    minus = [values[l] - values[7 - l] for l in range(HALF)]
    result = [None] * QUAD_POINT_TALLY
    for i in range(HALF):
        from_plus = sum(float(even[i, l]) * plus[l] for l in range(HALF))
        from_minus = sum(float(odd[i, l]) * minus[l] for l in range(HALF))
        result[i] = from_minus + from_plus
        result[7 - i] = from_minus - from_plus
    return result


def square_line(matrix, values):
    even, odd = line_tables(matrix)
    plus = [values[l] + values[7 - l] for l in range(HALF)]
    minus = [values[l] - values[7 - l] for l in range(HALF)]
    result = [None] * QUAD_POINT_TALLY
    for i in range(HALF):
        from_plus = sum(float(even[i, l]) * plus[l] for l in range(HALF))
        from_minus = sum(float(odd[i, l]) * minus[l] for l in range(HALF))
        result[i] = from_plus + from_minus
        result[7 - i] = from_plus - from_minus
    return result


def stacked_matrix(matrix):
    whole = matrix.astype(np.float32)
    high = whole.astype(jnp.bfloat16)
    low = (whole - high.astype(np.float32)).astype(jnp.bfloat16)
    return np.concatenate([high, low, high], axis=1)


def height_product(stacked, values):
    high = values.astype(jnp.bfloat16)
    low = (values - high.astype(jnp.float32)).astype(jnp.bfloat16)
    both = jnp.concatenate([high, high, low], axis=0)
    return jnp.dot(stacked, both, preferred_element_type=jnp.float32)


def rows_of(j):
    return slice(QUAD_POINT_TALLY * j, QUAD_POINT_TALLY * (j + 1))


def height_weights(shape):
    level = lax.broadcasted_iota(jnp.int32, shape, 0)
    result = jnp.full(shape, float(WEIGHTS[0]), jnp.float32)
    for k in range(1, QUAD_POINT_TALLY):
        result = jnp.where(level == k, float(WEIGHTS[k]), result)
    return result


def copy_weights(shape):
    level = lax.broadcasted_iota(jnp.int32, shape, 0)
    layer = lax.broadcasted_iota(jnp.int32, shape, 1)
    shared = ((level == 0) & (layer > 0)) | (
        (level == QUAD_POINT_TALLY - 1) & (layer < shape[1] - 1)
    )
    return jnp.where(shared, 0.5, 1.0)


def side_weight(i, j):
    return (0.5 if i in (0, 7) else 1.0) * (0.5 if j in (0, 7) else 1.0)


HEIGHT, SIDE, HEIGHT_BACK, HEIGHT_SQUARE = (slice(n * ROWS, (n + 1) * ROWS) for n in range(4))
BOTH = slice(0, 2 * ROWS)


def constants():
    one = np.eye(QUAD_POINT_TALLY)
    return jnp.asarray(
        np.concatenate([
            stacked_matrix(np.kron(one, DERIV)),
            stacked_matrix(np.kron(DERIV, one)),
            stacked_matrix(np.kron(one, DERIV.T)),
            stacked_matrix(np.kron(one, (DERIV * DERIV).T)),
        ])
    )


def dom_sides():
    odd = lax.rem(lax.axis_index("dom"), 2)
    return 7 * (1 - odd), 7 * odd


def batch_sides():
    odd = lax.rem(lax.axis_index("batch"), 2)
    return 1 - odd, odd


UPPER = pl.ds(QUAD_POINT_TALLY - 1, QUAD_POINT_TALLY, stride=QUAD_POINT_TALLY)
LOWER = pl.ds(0, QUAD_POINT_TALLY, stride=QUAD_POINT_TALLY)
TAIL = slice(LAST, ROWS)
HEAD = slice(0, QUAD_POINT_TALLY)


def sum_heights(field, slot):
    layers = field.shape[3]
    lane = lax.broadcasted_iota(jnp.int32, (QUAD_POINT_TALLY, layers), 1)
    for i in range(field.shape[0]):
        upper = field[i, slot, UPPER, :]
        lower = field[i, slot, LOWER, :]
        above = jnp.where(lane < layers - 1, pltpu.roll(lower, layers - 1, 1), 0.0)
        below = jnp.where(lane > 0, pltpu.roll(upper, 1, 1), 0.0)
        field[i, slot, UPPER, :] = upper + above
        field[i, slot, LOWER, :] = lower + below


def face_rows(b):
    return slice(b * LAST, b * LAST + ROWS)


class Parts:
    def __init__(self, inner, ends):
        self.inner, self.ends = inner, ends
        self.blocks = inner.shape[1] + 2

    def at(self, b):
        if b in (0, self.blocks - 1):
            return self.ends, min(b, 1)
        return self.inner, b - 1

    def load(self, i, b, rows):
        field, slot = self.at(b)
        return field[i, slot, rows, :]


class Sides(Parts):
    def load(self, i, b, rows):
        field, slot = self.at(b)
        plane = jnp.minimum(i, 1) if b in (0, self.blocks - 1) else i
        return field[plane, slot, rows, :]


class Whole:
    def __init__(self, field):
        self.field, self.blocks = field, field.shape[1]

    def load(self, i, b, rows):
        return self.field[i, b, rows, :]


def joined(parts, i, b, out):
    out[...] = parts.load(i, b, slice(0, ROWS))
    if b > 0:
        out[HEAD, :] = out[HEAD, :] + parts.load(i, b - 1, TAIL)
    if b < parts.blocks - 1:
        out[TAIL, :] = out[TAIL, :] + parts.load(i, b + 1, HEAD)


def emit_faces(parts, first, second):
    for side, target in zip(dom_sides(), (first, second)):
        for b in range(parts.blocks):
            joined(parts, side, b, target.at[face_rows(b)])


def emit_ends(parts, ends):
    for i in range(QUAD_POINT_TALLY):
        ends[0, i] = parts.load(i, 0, HEAD)
        ends[1, i] = parts.load(i, parts.blocks - 1, TAIL)


def assemble(parts, b, out, slot, dom_received, batch_received):
    for i in range(QUAD_POINT_TALLY):
        joined(parts, i, b, out.at[i, slot])
    for side, received in zip(dom_sides(), dom_received):
        out[side, slot] = out[side, slot] + received[face_rows(b), :]
    if batch_received is not None and b in (0, parts.blocks - 1):
        rows = HEAD if b == 0 else TAIL
        low, _ = batch_sides()
        from_first = low == (0 if b == 0 else 1)
        for i in range(QUAD_POINT_TALLY):
            received = jnp.where(from_first, batch_received[0][i], batch_received[1][i])
            out[i, slot, rows, :] = out[i, slot, rows, :] + received


def clear_top(field, slot, keep, b):
    for i in range(QUAD_POINT_TALLY):
        field[i, slot, UPPER, :] = field[i, slot, UPPER, :] * keep[i, b]


def apply_block(field, slot, metric, b, scratch_s, scratch_t, out, matrices, scale=1.0, extra=None):
    both, height_back = matrices[BOTH], matrices[HEIGHT_BACK]
    back = DERIV.T
    for i in range(QUAD_POINT_TALLY):
        slopes = height_product(both, field[i, slot])
        scratch_t[i] = slopes[:ROWS]
        scratch_s[i] = slopes[ROWS:]
    for j in range(QUAD_POINT_TALLY):
        rows = rows_of(j)
        along_r = deriv_line(DERIV, [field[i, slot, rows, :] for i in range(QUAD_POINT_TALLY)])
        flux_r = []
        additions = []
        for i in range(QUAD_POINT_TALLY):
            along_s, along_t = scratch_s[i, rows, :], scratch_t[i, rows, :]
            rr, ss, tt = (metric[n, i, b, rows, :] for n in range(3))
            rs, rt, st = (metric[n, i, b, rows, :] for n in range(3, 6))
            flux_r.append(rr * along_r[i] + rs * along_s + rt * along_t)
            scratch_s[i, rows, :] = rs * along_r[i] + ss * along_s + st * along_t
            scratch_t[i, rows, :] = rt * along_r[i] + st * along_s + tt * along_t
            if extra is not None:
                additions.append(extra(i, j, along_r[i], along_s, along_t))
        result = deriv_line(scale * back, flux_r)
        for i in range(QUAD_POINT_TALLY):
            out[i, slot, rows, :] = result[i] if extra is None else result[i] + additions[i]
    total = None
    for i in range(QUAD_POINT_TALLY):
        block = scratch_s[i]
        from_s = deriv_line(scale * back, [block[rows_of(j)] for j in range(QUAD_POINT_TALLY)])
        from_t = height_product(height_back, scratch_t[i])
        for j in range(QUAD_POINT_TALLY):
            rows = rows_of(j)
            term = from_t[rows] if scale == 1.0 else scale * from_t[rows]
            value = out[i, slot, rows, :] + from_s[j] + term
            out[i, slot, rows, :] = value
            if extra is None:
                term = field[i, slot, rows, :] * value
                total = term if total is None else total + term
    return total


def apply_faces(field, slot, metric, b, scratch_s, scratch_t, faces, matrices, scale=1.0, extra=None):
    both, height_back = matrices[BOTH], matrices[HEIGHT_BACK]
    back = DERIV.T
    even, odd = line_tables(scale * back)
    for i in range(QUAD_POINT_TALLY):
        slopes = height_product(both, field[i, slot])
        scratch_t[i] = slopes[:ROWS]
        scratch_s[i] = slopes[ROWS:]
    for j in range(QUAD_POINT_TALLY):
        rows = rows_of(j)
        along_r = deriv_line(DERIV, [field[i, slot, rows, :] for i in range(QUAD_POINT_TALLY)])
        flux_r = []
        additions = {}
        for i in range(QUAD_POINT_TALLY):
            along_s, along_t = scratch_s[i, rows, :], scratch_t[i, rows, :]
            rr, rs, rt = (metric[n, i, b, rows, :] for n in (0, 3, 4))
            flux_r.append(rr * along_r[i] + rs * along_s + rt * along_t)
            if i in (0, 7):
                ss, tt, st = (metric[n, i, b, rows, :] for n in (1, 2, 5))
                scratch_s[i, rows, :] = rs * along_r[i] + ss * along_s + st * along_t
                scratch_t[i, rows, :] = rt * along_r[i] + st * along_s + tt * along_t
                if extra is not None:
                    additions[i] = extra(i, j, along_r[i], along_s, along_t)
        common = sum(float(odd[0, l]) * (flux_r[l] - flux_r[7 - l]) for l in range(HALF))
        change = sum(float(even[0, l]) * (flux_r[l] + flux_r[7 - l]) for l in range(HALF))
        for n, i in enumerate((0, 7)):
            value = common + change if i == 0 else common - change
            faces[n, slot, rows, :] = value if extra is None else value + additions[i]
    for n, i in enumerate((0, 7)):
        block = scratch_s[i]
        from_s = deriv_line(scale * back, [block[rows_of(j)] for j in range(QUAD_POINT_TALLY)])
        from_t = height_product(height_back, scratch_t[i])
        for j in range(QUAD_POINT_TALLY):
            rows = rows_of(j)
            term = from_t[rows] if scale == 1.0 else scale * from_t[rows]
            faces[n, slot, rows, :] = faces[n, slot, rows, :] + from_s[j] + term


def dot_weighted(left, right, slot):
    layers = left.shape[3]
    sums = {}
    for i in range(QUAD_POINT_TALLY):
        for j in range(QUAD_POINT_TALLY):
            weight = side_weight(i, j)
            term = left[i, slot, rows_of(j), :] * right[i, slot, rows_of(j), :]
            sums[weight] = sums[weight] + term if weight in sums else term
    total = sums[1.0] + 0.5 * sums[0.5] + 0.25 * sums[0.25]
    return total * copy_weights((QUAD_POINT_TALLY, layers))


def mass_faces_kernel(
    determinant, prior, first, second, ends, prior_ends, det_face, det_end, prior_face, prior_end,
    mass_face, mass_end, sems,
):
    blocks, layers = determinant.shape[1], first.shape[2]
    last = blocks - 1
    copies = []
    for n, i in enumerate((0, 7)):
        copies.append((determinant.at[i], det_face.at[n]))
        copies.append((prior.at[i], prior_face.at[n]))
    for n, (b, j) in enumerate(((0, 0), (last, 7))):
        copies.append((determinant.at[:, b, j], det_end.at[n]))
        copies.append((prior.at[:, b, j], prior_end.at[n]))
    started = [
        pltpu.make_async_copy(source, target, sems.at[n])
        for n, (source, target) in enumerate(copies)
    ]
    for copy in started:
        copy.start()
    for copy in started:
        copy.wait()
    weights = height_weights((QUAD_POINT_TALLY, layers))
    for n, i in enumerate((0, 7)):
        for b in range(blocks):
            for j in range(QUAD_POINT_TALLY):
                weight = weights * float(WEIGHTS[i] * WEIGHTS[j])
                value = weight * det_face[n, b, j].astype(jnp.float32)
                mass_face[0, n, b, rows_of(j), :] = value
                mass_face[1, n, b, rows_of(j), :] = value * prior_face[n, b, j]
    for side, j in enumerate((0, 7)):
        for i in range(QUAD_POINT_TALLY):
            weight = weights * float(WEIGHTS[i] * WEIGHTS[j])
            value = weight * det_end[side, i].astype(jnp.float32)
            mass_end[0, 0, side, rows_of(i), :] = value
            mass_end[1, 0, side, rows_of(i), :] = value * prior_end[side, i]
    for n in range(2):
        for b in range(blocks):
            sum_heights(mass_face.at[n], b)
        for side in range(2):
            sum_heights(mass_end.at[n], side)
            for i in range(QUAD_POINT_TALLY):
                (ends, prior_ends)[n][0, side, i] = mass_end[n, 0, side, rows_of(i), :]
        for b in range(blocks - 1):
            for face in range(2):
                total = mass_face[n, face, b, TAIL, :] + mass_face[n, face, b + 1, HEAD, :]
                mass_face[n, face, b, TAIL, :] = total
                mass_face[n, face, b + 1, HEAD, :] = total
        odd, _ = dom_sides()
        face_first = jnp.minimum(odd, 1)
        for b in range(blocks):
            first[n, face_rows(b), :] = mass_face[n, face_first, b]
            second[n, face_rows(b), :] = mass_face[n, 1 - face_first, b]


def prepare_kernel(
    determinant, prior, pure, mixed, matrices, mass, mass_prior, metric, diagonal,
    det_in, prior_in, pure_in, mixed_in, sems,
):
    blocks, layers = diagonal.shape[1], diagonal.shape[3]
    weights = height_weights((QUAD_POINT_TALLY, layers))
    level = lax.broadcasted_iota(jnp.int32, (QUAD_POINT_TALLY, layers), 0)
    ends = [float(DERIV[i, i]) for i in range(QUAD_POINT_TALLY)]
    height_ends = jnp.where(level == 0, ends[0], jnp.where(level == 7, ends[7], 0.0))
    squares = DERIV * DERIV

    def mass_copies(b):
        return (
            pltpu.make_async_copy(determinant.at[:, b], det_in.at[:, b], sems.at[0, b]),
            pltpu.make_async_copy(prior.at[:, b], prior_in.at[:, b], sems.at[1, b]),
        )

    def metric_copies(b):
        return (
            pltpu.make_async_copy(pure.at[:, :, b], pure_in.at[:, :, b], sems.at[2, b]),
            pltpu.make_async_copy(mixed.at[:, :, b], mixed_in.at[:, :, b], sems.at[3, b]),
        )

    for copies in (mass_copies, metric_copies):
        for b in range(blocks):
            for copy in copies(b):
                copy.start()

    def mass_block(b, carry):
        for copy in mass_copies(b):
            copy.wait()
        for i in range(QUAD_POINT_TALLY):
            for j in range(QUAD_POINT_TALLY):
                weight = weights * float(WEIGHTS[i] * WEIGHTS[j])
                value = weight * det_in[i, b, j].astype(jnp.float32)
                mass[i, b, rows_of(j), :] = value
                mass_prior[i, b, rows_of(j), :] = value * prior_in[i, b, j]
        sum_heights(mass, b)
        sum_heights(mass_prior, b)
        return carry

    def metric_block(b, carry):
        for copy in metric_copies(b):
            copy.wait()
        for i in range(QUAD_POINT_TALLY):
            for j in range(QUAD_POINT_TALLY):
                weight = weights * float(WEIGHTS[i] * WEIGHTS[j])
                for n in range(3):
                    metric[n, i, b, rows_of(j), :] = weight * pure_in[n, i, b, j].astype(
                        jnp.float32
                    )
                    metric[n + 3, i, b, rows_of(j), :] = weight * mixed_in[n, i, b, j].astype(
                        jnp.float32
                    )
        for j in range(QUAD_POINT_TALLY):
            line = square_line(
                squares.T, [metric[0, i, b, rows_of(j), :] for i in range(QUAD_POINT_TALLY)]
            )
            for i in range(QUAD_POINT_TALLY):
                diagonal[i, b, rows_of(j), :] = line[i]
        for i in range(QUAD_POINT_TALLY):
            line = square_line(
                squares.T, [metric[1, i, b, rows_of(j), :] for j in range(QUAD_POINT_TALLY)]
            )
            from_t = height_product(matrices[HEIGHT_SQUARE], metric[2, i, b])
            for j in range(QUAD_POINT_TALLY):
                rows = rows_of(j)
                value = diagonal[i, b, rows, :] + line[j] + from_t[rows]
                if ends[i] != 0.0 and ends[j] != 0.0:
                    value = value + (2.0 * ends[i] * ends[j]) * metric[3, i, b, rows, :]
                if ends[i] != 0.0:
                    value = value + (2.0 * ends[i]) * height_ends * metric[4, i, b, rows, :]
                if ends[j] != 0.0:
                    value = value + (2.0 * ends[j]) * height_ends * metric[5, i, b, rows, :]
                diagonal[i, b, rows, :] = value
        sum_heights(diagonal, b)
        return carry

    lax.fori_loop(0, blocks, mass_block, 0)
    lax.fori_loop(0, blocks, metric_block, 0)


def source_kernel(
    metric, heat, wind, determinant, diagonal, matrices,
    numerator, first, second, diag_ends, heat_ends, scratch_s, scratch_t,
):
    blocks, layers = numerator.shape[1], numerator.shape[3]
    weights = height_weights((QUAD_POINT_TALLY, layers))

    def block(b, carry):
        def extra(i, j, along_r, along_s, along_t):
            weight = weights * float(WEIGHTS[i] * WEIGHTS[j])
            convection = (
                wind[0, i, b, j].astype(jnp.float32) * along_r
                + wind[1, i, b, j].astype(jnp.float32) * along_s
                + wind[2, i, b, j].astype(jnp.float32) * along_t
            )
            return weight * (
                determinant[i, b, j].astype(jnp.float32) * heat[i, b, rows_of(j), :]
                - transport_increment * convection
            )

        apply_block(
            heat, b, metric, b, scratch_s, scratch_t, numerator, matrices,
            -conduction_increment, extra,
        )
        sum_heights(numerator, b)
        return carry

    lax.fori_loop(0, blocks, block, 0)
    for n, (field, ends) in enumerate(((diagonal, diag_ends), (numerator, heat_ends))):
        emit_faces(Whole(field), first.at[n], second.at[n])
        emit_ends(Whole(field), ends.at[0])


def ends_kernel(offsets, *refs):
    inputs, (first, second) = refs[: 3 * len(offsets)], refs[3 * len(offsets) :]
    for n, offset in enumerate(offsets):
        ends, *received = inputs[3 * n : 3 * n + 3]
        last = received[0].shape[1] - QUAD_POINT_TALLY
        for side, target in zip(batch_sides(), (first, second)):
            rows = pl.ds(pl.multiple_of(side * last, QUAD_POINT_TALLY), QUAD_POINT_TALLY)
            for i in range(QUAD_POINT_TALLY):
                target[n, i] = ends[0, side, i]
            for dom_side, face in zip(dom_sides(), received):
                target[n, dom_side] = target[n, dom_side] + face[offset, rows, :]


def elements(inner, blocks):
    return list(enumerate(range(1, blocks - 1) if inner else (0, blocks - 1)))


class Sending:
    def __init__(self, sems):
        self.sems, self.copies = sems, []

    def start(self, source, target):
        copy = pltpu.make_async_copy(source, target, self.sems.at[len(self.copies)])
        copy.start()
        self.copies.append(copy)

    def wait(self):
        for copy in self.copies:
            copy.wait()


def start_source(determinant, spread, b):
    layers = spread.shape[3]
    weights = height_weights((QUAD_POINT_TALLY, layers))

    def extra(i, j, along_r, along_s, along_t):
        weight = weights * float(-WEIGHTS[i] * WEIGHTS[j] / step_dt)
        return (weight * determinant[i, b, j].astype(jnp.float32)) * spread[i, b, rows_of(j), :]

    return extra


def assemble_head(mass, mass_prior, dom, batch, keep, slot, b, mass_inverse, head):
    for n, (field, out) in enumerate(((mass, mass_inverse), (mass_prior, head))):
        assemble(
            Whole(field), b, out, slot, tuple(face.at[n] for face in dom),
            batch and tuple(face.at[n] for face in batch),
        )
    clear_top(head, slot, keep, b)
    for i in range(QUAD_POINT_TALLY):
        inverse = 1.0 / mass_inverse[i, slot]
        mass_inverse[i, slot] = inverse
        head[i, slot] = head[i, slot] * inverse


def start_inner_kernel(
    mass, mass_prior, dom_first, dom_second, metric, spread, determinant, keep, matrices,
    head_out, mass_inverse, residual, scratch_s, scratch_t, head, sems,
):
    blocks = mass.shape[1]
    sending = Sending(sems)
    for slot, b in elements(True, blocks):
        assemble_head(
            mass, mass_prior, (dom_first, dom_second), None, keep, slot, b, mass_inverse, head
        )
        sending.start(head.at[:, slot], head_out.at[:, slot])
        apply_block(
            head, slot, metric, b, scratch_s, scratch_t, residual, matrices, -1.0,
            start_source(determinant, spread, b),
        )
        sum_heights(residual, slot)
    sending.wait()


def start_faces_kernel(
    mass, mass_prior, dom_first, dom_second, batch_first, batch_second,
    metric, spread, determinant, keep, matrices, residual_inner,
    head, mass_inverse, first, second, scratch_s, scratch_t, faces,
):
    blocks = mass.shape[1]
    for slot, b in elements(False, blocks):
        assemble_head(
            mass, mass_prior, (dom_first, dom_second), (batch_first, batch_second), keep,
            slot, b, mass_inverse, head,
        )
        apply_faces(
            head, slot, metric, b, scratch_s, scratch_t, faces, matrices, -1.0,
            start_source(determinant, spread, b),
        )
        sum_heights(faces, slot)
    emit_faces(Sides(residual_inner, faces), first.at[0], second.at[0])


def start_ends_kernel(
    head, metric, spread, determinant, matrices, residual_inner,
    head_out, residual, ends, scratch_s, scratch_t, sems,
):
    sending = Sending(sems)
    sending.start(head, head_out)
    for slot, b in elements(False, metric.shape[2]):
        apply_block(
            head, slot, metric, b, scratch_s, scratch_t, residual, matrices, -1.0,
            start_source(determinant, spread, b),
        )
        sum_heights(residual, slot)
    emit_ends(Parts(residual_inner, residual), ends.at[0])
    sending.wait()


def row_sums(*parts):
    rows = [jnp.sum(part, axis=0, keepdims=True) for part in parts]
    rows.append(jnp.zeros((QUAD_POINT_TALLY - len(parts), parts[0].shape[1]), jnp.float32))
    return jnp.concatenate(rows, axis=0)


def assemble_direction(
    residual_parts, diagonal, res_dom, diag_dom, batch, keep, slot, b,
    residual, diag_inverse, direction,
):
    assemble(
        residual_parts, b, residual, slot, tuple(face.at[0] for face in res_dom),
        batch and tuple(face.at[0] for face in batch),
    )
    assemble(
        Whole(diagonal), b, diag_inverse, slot, tuple(face.at[0] for face in diag_dom),
        batch and tuple(face.at[1] for face in batch),
    )
    clear_top(residual, slot, keep, b)
    for i in range(QUAD_POINT_TALLY):
        inverse = 1.0 / diag_inverse[i, slot]
        diag_inverse[i, slot] = inverse
        direction[i, slot] = residual[i, slot] * inverse


def apply_dots(left, field, inner, metric, scratch_s, scratch_t, out, matrices):
    energy = product = 0.0
    for slot, b in elements(inner, metric.shape[2]):
        energy += apply_block(field, slot, metric, b, scratch_s, scratch_t, out, matrices)
        product += dot_weighted(left, field, slot)
        sum_heights(out, slot)
    return product, energy


def first_inner_kernel(
    residual_inner, residual_ends, diagonal, res_first, res_second, diag_first, diag_second,
    metric, keep, matrices,
    direction_out, diag_inverse, image, dots, scratch_s, scratch_t, residual, direction, sems,
):
    sending = Sending(sems)
    for slot, b in elements(True, diagonal.shape[1]):
        assemble_direction(
            Parts(residual_inner, residual_ends), diagonal, (res_first, res_second),
            (diag_first, diag_second), None, keep, slot, b, residual, diag_inverse, direction,
        )
        sending.start(direction.at[:, slot], direction_out.at[:, slot])
    dots[...] = row_sums(
        *apply_dots(residual, direction, True, metric, scratch_s, scratch_t, image, matrices)
    )
    sending.wait()


def first_faces_kernel(
    residual_inner, residual_ends, diagonal, res_first, res_second, diag_first, diag_second,
    batch_first, batch_second, metric, keep, matrices, image_inner,
    direction, residual, diag_inverse, first, second, scratch_s, scratch_t, faces,
):
    for slot, b in elements(False, diagonal.shape[1]):
        assemble_direction(
            Parts(residual_inner, residual_ends), diagonal, (res_first, res_second),
            (diag_first, diag_second), (batch_first, batch_second), keep, slot, b,
            residual, diag_inverse, direction,
        )
        apply_faces(direction, slot, metric, b, scratch_s, scratch_t, faces, matrices)
        sum_heights(faces, slot)
    emit_faces(Sides(image_inner, faces), first.at[0], second.at[0])


def first_ends_kernel(
    direction, residual, metric, matrices, image_inner, dots_inner,
    direction_out, image, ends, dots, scratch_s, scratch_t, sems,
):
    sending = Sending(sems)
    sending.start(direction, direction_out)
    dots[...] = dots_inner[...] + row_sums(
        *apply_dots(residual, direction, False, metric, scratch_s, scratch_t, image, matrices)
    )
    emit_ends(Parts(image_inner, image), ends.at[0])
    sending.wait()


def second_inner_kernel(
    image_inner, image_ends, dom_first, dom_second, diag_inverse, metric, keep, matrices, dots_in,
    scaled_out, image_two, dots, scratch_s, scratch_t, image, scaled, sems,
):
    parts = Parts(image_inner, image_ends)
    sending = Sending(sems)
    for slot, b in elements(True, parts.blocks):
        assemble(parts, b, image, slot, (dom_first.at[0], dom_second.at[0]), None)
        clear_top(image, slot, keep, b)
        for i in range(QUAD_POINT_TALLY):
            scaled[i, slot] = image[i, slot] * diag_inverse[i, slot]
        sending.start(scaled.at[:, slot], scaled_out.at[:, slot])
    product, energy = apply_dots(
        image, scaled, True, metric, scratch_s, scratch_t, image_two, matrices
    )
    nothing = jnp.zeros_like(energy)
    dots[...] = dots_in[...] + row_sums(nothing, nothing, product, energy)
    sending.wait()


def second_ends_kernel(
    image_inner, image_ends, dom_first, dom_second, batch_first, batch_second,
    diag_inverse, metric, keep, matrices, two_inner, dots_in,
    scaled_out, image_two, first, second, ends, all_dots,
    scratch_s, scratch_t, image, scaled, sems,
):
    parts = Parts(image_inner, image_ends)
    sending = Sending(sems)
    for slot, b in elements(False, parts.blocks):
        assemble(
            parts, b, image, slot, (dom_first.at[0], dom_second.at[0]),
            (batch_first.at[0], batch_second.at[0]),
        )
        clear_top(image, slot, keep, b)
        for i in range(QUAD_POINT_TALLY):
            scaled[i, slot] = image[i, slot] * diag_inverse[i, slot]
        sending.start(scaled.at[:, slot], scaled_out.at[:, slot])
    product, energy = apply_dots(
        image, scaled, False, metric, scratch_s, scratch_t, image_two, matrices
    )
    nothing = jnp.zeros_like(energy)
    sums = dots_in[...] + row_sums(nothing, nothing, product, energy)
    for n in range(all_dots.shape[0]):
        all_dots[n] = sums
    emit_faces(Parts(two_inner, image_two), first.at[0], second.at[0])
    emit_ends(Parts(two_inner, image_two), ends.at[0])
    sending.wait()


def heat_kernel(
    numerator, dom_first, dom_second, inverse_inner, inverse_ends, heat, values, factors
):
    blocks = heat.shape[1]
    inverse = Parts(inverse_inner, inverse_ends)
    for b in range(blocks):
        assemble(Whole(numerator), b, heat, b, (dom_first.at[1], dom_second.at[1]), None)
        for i in range(QUAD_POINT_TALLY):
            heat[i, b] = heat[i, b] * inverse.load(i, b, slice(0, ROWS))
    for side, (b, rows) in enumerate(((0, HEAD), (blocks - 1, TAIL))):
        for i in range(QUAD_POINT_TALLY):
            values[side, i] = heat[i, b, rows, :]
            factors[side, i] = inverse.load(i, b, rows)


CHUNK = 1


def last_kernel(
    image_inner, image_ends, dom_first, dom_second, diag_inner, diag_ends, keep, all_dots,
    head_inner, head_ends, direction_inner, direction_ends, scaled_inner, scaled_ends,
    out_head, out_defect, end_values, end_factors,
    image, far, result_head, result_defect, sems_in, sems_out,
):
    sources = (
        head_inner, head_ends, direction_inner, direction_ends, scaled_inner, scaled_ends
    )
    chunks = QUAD_POINT_TALLY // CHUNK
    arriving = []
    for c in range(chunks):
        planes = pl.ds(c * CHUNK, CHUNK)
        arriving.append([
            pltpu.make_async_copy(
                source.at[planes], far.at[n // 2, n % 2, planes], sems_in.at[c, n]
            )
            for n, source in enumerate(sources)
        ])
        for copy in arriving[-1]:
            copy.start()
    parts, inverses = Parts(image_inner, image_ends), Parts(diag_inner, diag_ends)
    blocks, layers = parts.blocks, image.shape[3]
    level = lax.broadcasted_iota(jnp.int32, (QUAD_POINT_TALLY, layers), 0)
    sums = all_dots[0]
    for n in range(1, all_dots.shape[0]):
        sums = sums + all_dots[n]
    sums = jnp.sum(sums, axis=1, keepdims=True)
    inner, energy, cross, energy_two = (sums[n : n + 1] for n in range(4))
    step = inner / energy
    following = step * step * cross - inner
    growth = 1.0 + following / inner
    curvature = growth * growth * energy - 2.0 * growth * step * cross + step * step * energy_two
    step_two = following / curvature
    along_direction = step + step_two * growth
    along_scaled = step * step_two
    whole = slice(0, ROWS)
    for b in range(blocks):
        for i in range(QUAD_POINT_TALLY):
            joined(parts, i, b, image.at[i, b])
        for side, received in zip(dom_sides(), (dom_first, dom_second)):
            image[side, b] = image[side, b] + received[0, face_rows(b), :]
        clear_top(image, b, keep, b)
    leaving = []
    for c in range(chunks):
        planes = pl.ds(c * CHUNK, CHUNK)
        for copy in arriving[c]:
            copy.wait()
        for i in range(c * CHUNK, (c + 1) * CHUNK):
            for b in range(blocks):
                kind, slot = (1, min(b, 1)) if b in (0, blocks - 1) else (0, b - 1)
                start, change = far[1, kind, i, slot], far[2, kind, i, slot]
                inverse = inverses.load(i, b, whole)
                result_head[i, b] = (
                    far[0, kind, i, slot] + along_direction * start - along_scaled * change
                )
                result_defect[i, b] = (
                    start - along_direction * change + along_scaled * (image[i, b] * inverse)
                )
            for side, (b, j) in enumerate(((0, 0), (blocks - 1, 7))):
                end_values[side, i] = result_defect[i, b, rows_of(j), :]
                top = jnp.where(level == 7, keep[i, b, j : j + 1, :], 1.0)
                end_factors[side, i] = along_scaled * top * inverses.load(i, b, rows_of(j))
        for n, (source, target) in enumerate(
            ((result_head, out_head), (result_defect, out_defect))
        ):
            copy = pltpu.make_async_copy(source.at[planes], target.at[planes], sems_out.at[c, n])
            copy.start()
            leaving.append(copy)
    for copy in leaving:
        copy.wait()


def close_kernel(
    defect, heat, batch_first, batch_second, defect_values, defect_factors, heat_values,
    heat_factors, out_defect, out_heat, rows, sems,
):
    del defect, heat
    low, _ = batch_sides()
    copies = []
    for n, (values, factors, out) in enumerate((
        (defect_values, defect_factors, out_defect), (heat_values, heat_factors, out_heat)
    )):
        for side, (b, start) in enumerate(((0, 0), (out.shape[1] - 1, LAST))):
            for i in range(QUAD_POINT_TALLY):
                received = jnp.where(low == side, batch_first[n, i], batch_second[n, i])
                rows[n, side, i] = values[side, i] + factors[side, i] * received
            copy = pltpu.make_async_copy(
                rows.at[n, side], out.at[:, b, pl.ds(start, QUAD_POINT_TALLY), :],
                sems.at[n, side],
            )
            copy.start()
            copies.append(copy)
    for copy in copies:
        copy.wait()


COST = {
    "mass_faces": 2, "prepare": 10, "source": 14, "start_inner": 8, "start_faces": 4,
    "start_ends": 8, "first_inner": 8, "first_faces": 4, "first_ends": 6, "heat": 4,
    "second_inner": 8, "second_ends": 8, "last": 12, "close": 2,
}


def call(kernel, name, outs, args, scratch=(), far_in=(), far_out=(), aliases=None):
    near, far = pl.BlockSpec(memory_space=pltpu.VMEM), pl.BlockSpec(memory_space=pltpu.HBM)
    args = [
        pltpu.with_memory_space_constraint(arg, pltpu.HBM) if n in far_in else arg
        for n, arg in enumerate(args)
    ]
    return pl.pallas_call(
        kernel,
        name=name,
        out_shape=[
            (pltpu.HBM if n in far_out else jax.ShapeDtypeStruct)(shape, jnp.float32)
            for n, shape in enumerate(outs)
        ],
        in_specs=[far if n in far_in else near for n in range(len(args))],
        out_specs=[far if n in far_out else near for n in range(len(outs))],
        scratch_shapes=[
            shape if not isinstance(shape, tuple) else pltpu.VMEM(shape, jnp.float32)
            for shape in scratch
        ],
        input_output_aliases=aliases or {},
        cost_estimate=pl.CostEstimate(
            flops=0, bytes_accessed=COST.get(name, 0) * 1000000, transcendentals=0
        ),
        compiler_params=pltpu.CompilerParams(vmem_limit_bytes=VMEM_LIMIT),
    )(*args)


def swaps(first, second, axis):
    count = lax.axis_size(axis)
    near = [(index, index ^ 1) for index in range(count)]
    far = [(index, (((index + 1) ^ 1) - 1) % count) for index in range(count)]
    second = lax.ppermute(second, axis, far)
    return lax.ppermute(first, axis, near), second


def shards(
    heat_state_element,
    wind_reference_flux,
    geometric_pure_factors,
    geometric_mixed_factors,
    mapping_determinant,
    velocity_source_spread,
    prior_head_state,
    exit_boundary_marks,
):
    _, points, blocks, _, _, layers = heat_state_element.shape
    block_shape = (points, blocks, ROWS, layers)
    inner_shape = (points, blocks - 2, ROWS, layers)
    ends_shape = (points, 2, ROWS, layers)
    heat = heat_state_element.reshape(block_shape)
    spread = velocity_source_spread.reshape(block_shape)
    prior = prior_head_state[0]
    wind, pure, mixed = (
        array.reshape(array.shape[:1] + array.shape[2:])
        for array in (wind_reference_flux, geometric_pure_factors, geometric_mixed_factors)
    )
    determinant = mapping_determinant[0]
    layer = lax.broadcasted_iota(jnp.int32, (points, blocks, points, layers), 3)
    marks = exit_boundary_marks[0].astype(jnp.float32)[:, :, :, None]
    keep = jnp.where(layer == layers - 1, 1.0 - marks, 1.0)
    matrices = constants()

    end_shape = (1, 2, points, points, layers)

    def faces(count):
        return [(count, blocks * LAST + QUAD_POINT_TALLY, layers)] * 2

    def ends_call(name, *groups):
        return call(
            functools.partial(ends_kernel, [group[-1] for group in groups]),
            name,
            [(len(groups), points, points, layers)] * 2,
            [array for group in groups for array in group[:-1]],
        )

    pair = [(points, ROWS, layers)] * 2
    plane = (points, layers)
    side_shape = (2, 2, ROWS, layers)

    *mass_faces, mass_ends, prior_ends = call(
        mass_faces_kernel, "mass_faces", faces(2) + [end_shape] * 2, [determinant, prior],
        [
            pltpu.VMEM((2, blocks, points, points, layers), jnp.bfloat16),
            pltpu.VMEM((2, points, points, layers), jnp.bfloat16),
            (2, blocks, points, points, layers),
            (2, points, points, layers),
            (2, 2, blocks, ROWS, layers),
            (2, 1, 2, ROWS, layers),
            pltpu.SemaphoreType.DMA((8,)),
        ],
        far_in=(0, 1),
    )
    mass_dom = swaps(*mass_faces, "dom")
    mass, mass_prior, metric, diagonal = call(
        prepare_kernel, "prepare", [block_shape] * 2 + [(6,) + block_shape, block_shape],
        [determinant, prior, pure, mixed, matrices],
        [
            pltpu.VMEM(determinant.shape, jnp.bfloat16),
            prior.shape,
            pltpu.VMEM(pure.shape, jnp.bfloat16),
            pltpu.VMEM(mixed.shape, jnp.bfloat16),
            pltpu.SemaphoreType.DMA((4, blocks)),
        ],
        far_in=range(4),
    )
    numerator, *source_faces, diag_end, heat_end = call(
        source_kernel, "source", [block_shape] + faces(2) + [end_shape] * 2,
        [metric, heat, wind, determinant, diagonal, matrices], pair,
    )
    source_dom = swaps(*source_faces, "dom")
    mass_batch = swaps(
        *ends_call("mass_ends", (mass_ends, *mass_dom, 0), (prior_ends, *mass_dom, 1)), "batch"
    )
    sems = pltpu.SemaphoreType.DMA
    common = [metric, spread, determinant]
    head_inner, inverse_inner, residual_inner = call(
        start_inner_kernel, "start_inner", [inner_shape] * 3,
        [mass, mass_prior, *mass_dom, *common, keep, matrices],
        pair + [inner_shape, sems((blocks,))], far_out=(0,),
    )
    head_near, inverse_ends, *res_faces = call(
        start_faces_kernel, "start_faces", [ends_shape] * 2 + faces(1),
        [mass, mass_prior, *mass_dom, *mass_batch, *common, keep, matrices, residual_inner],
        pair + [side_shape],
    )
    res_dom = swaps(*res_faces, "dom")
    head_ends, residual_ends, res_ends = call(
        start_ends_kernel, "start_ends", [ends_shape] * 2 + [end_shape],
        [head_near, *common, matrices, residual_inner], pair + [sems((1,))], far_out=(0,),
    )
    res_batch = swaps(
        *ends_call("res_ends", (res_ends, *res_dom, 0), (diag_end, *source_dom, 0)), "batch"
    )
    residual = [residual_inner, residual_ends, diagonal, *res_dom, *source_dom]
    direction_inner, diag_inner, image_inner, dots_inner = call(
        first_inner_kernel, "first_inner", [inner_shape] * 3 + [plane],
        [*residual, metric, keep, matrices], pair + [inner_shape] * 2 + [sems((blocks,))],
        far_out=(0,),
    )
    direction_near, residual_near, diag_ends, *image_faces = call(
        first_faces_kernel, "first_faces", [ends_shape] * 3 + faces(1),
        [*residual, *res_batch, metric, keep, matrices, image_inner], pair + [side_shape],
    )
    image_dom = swaps(*image_faces, "dom")
    direction_ends, image_ends, image_out, dots = call(
        first_ends_kernel, "first_ends", [ends_shape] * 2 + [end_shape] + [plane],
        [direction_near, residual_near, metric, matrices, image_inner, dots_inner],
        pair + [sems((1,))], far_out=(0,),
    )
    heat_next, heat_values, heat_factors = call(
        heat_kernel, "heat", [block_shape] + [(2, points) + plane] * 2,
        [numerator, *source_dom, inverse_inner, inverse_ends],
    )
    heat_next, image_out = lax.optimization_barrier((heat_next, image_out))
    image_batch = swaps(*ends_call("image_ends", (image_out, *image_dom, 0)), "batch")
    count = lax.axis_size("dom") * lax.axis_size("batch")
    image = [image_inner, image_ends, *image_dom]
    scaled_inner, two_inner, dots = call(
        second_inner_kernel, "second_inner", [inner_shape] * 2 + [plane],
        [*image, diag_inner, metric, keep, matrices, dots],
        pair + [inner_shape] * 2 + [sems((blocks,))], far_out=(0,),
    )
    scaled_ends, two_ends, *two_faces, two_out, all_dots = call(
        second_ends_kernel, "second_ends",
        [ends_shape] * 2 + faces(1) + [end_shape, (count,) + plane],
        [*image, *image_batch, diag_ends, metric, keep, matrices, two_inner, dots],
        pair + [ends_shape] * 2 + [sems((2,))], far_out=(0,),
    )
    all_dots = lax.all_to_all(all_dots, ("dom", "batch"), 0, 0)
    two_dom = swaps(*two_faces, "dom")
    two_batch = swaps(
        *ends_call("two_ends", (two_out, *two_dom, 0), (heat_end, *source_dom, 1)), "batch"
    )
    chunks = points // CHUNK
    head_next, defect, end_values, end_factors = call(
        last_kernel, "last", [block_shape] * 2 + [(2, points) + plane] * 2,
        [two_inner, two_ends, *two_dom, diag_inner, diag_ends, keep, all_dots,
         head_inner, head_ends, direction_inner, direction_ends, scaled_inner, scaled_ends],
        [block_shape, (3, 2) + ends_shape, block_shape, block_shape,
         sems((chunks, 6)), sems((chunks, 2))],
        far_in=range(8, 14), far_out=(0, 1),
    )
    defect, heat_next = call(
        close_kernel, "close", [block_shape] * 2,
        [defect, heat_next, *two_batch, end_values, end_factors, heat_values, heat_factors],
        [(2, 2, points) + plane, sems((2, 2))],
        far_in=(0, 1), far_out=(0, 1), aliases={0: 0, 1: 1},
    )
    shape = heat_state_element.shape
    return heat_next.reshape(shape), head_next.reshape(shape), defect.reshape(shape)


def solution(mesh):
    field = P("dom", None, "batch", None, None, None)
    triple = P(None, "dom", None, "batch", None, None, None)
    return jax.shard_map(
        shards,
        mesh=mesh,
        in_specs=(
            field, triple, triple, triple, field, field, field, P("dom", None, "batch", None),
        ),
        out_specs=(field, field, field),
        check_vma=False,
    )
```

```python
import functools
import math

import jax
import jax.numpy as jnp
import numpy as np
from jax import lax
from jax.experimental import pallas as pl
from jax.experimental.pallas import tpu as pltpu
from jax.sharding import PartitionSpec as P

QUAD_POINT_TALLY = 8
ROWS = QUAD_POINT_TALLY * QUAD_POINT_TALLY
LAST = ROWS - QUAD_POINT_TALLY
ITERS = 2

transport_increment = 0.02
conduction_increment = 0.002
step_dt = 0.02

VMEM_LIMIT = 12 * 1024 * 1024


def legendre_pair(order, point):
    before, current = (1.0, point)
    for level in range(2, order + 1):
        before, current = (
            current,
            ((2 * level - 1) * point * current - (level - 1) * before) / level,
        )
    return (current, before)


def tables():
    degree = QUAD_POINT_TALLY - 1
    points = [math.cos(math.pi * index / degree) for index in range(QUAD_POINT_TALLY)]
    for sweep in range(60):
        updated = []
        for point in points:
            top_value, below_value = legendre_pair(degree, point)
            updated.append(
                point - (point * top_value - below_value) / (QUAD_POINT_TALLY * top_value)
            )
        points = updated
    nodes = points[::-1]
    values = [legendre_pair(degree, point)[0] for point in nodes]
    weights = [2.0 / (degree * QUAD_POINT_TALLY * value * value) for value in values]
    deriv = np.zeros((QUAD_POINT_TALLY, QUAD_POINT_TALLY))
    for row in range(QUAD_POINT_TALLY):
        for col in range(QUAD_POINT_TALLY):
            if row != col:
                deriv[row, col] = values[row] / values[col] / (nodes[row] - nodes[col])
    corner_value = degree * QUAD_POINT_TALLY / 4.0
    deriv[0, 0] = -corner_value
    deriv[degree, degree] = corner_value
    return deriv, np.array(weights)


DERIV, WEIGHTS = tables()
HALF = QUAD_POINT_TALLY // 2


def line_tables(matrix):
    flipped = matrix[:, ::-1]
    even = (matrix + flipped)[:HALF, :HALF] / 2
    odd = (matrix - flipped)[:HALF, :HALF] / 2
    return even, odd


def deriv_line(matrix, values):
    even, odd = line_tables(matrix)
    plus = [values[l] + values[7 - l] for l in range(HALF)]
    minus = [values[l] - values[7 - l] for l in range(HALF)]
    result = [None] * QUAD_POINT_TALLY
    for i in range(HALF):
        from_plus = sum(float(even[i, l]) * plus[l] for l in range(HALF))
        from_minus = sum(float(odd[i, l]) * minus[l] for l in range(HALF))
        result[i] = from_minus + from_plus
        result[7 - i] = from_minus - from_plus
    return result


def square_line(matrix, values):
    even, odd = line_tables(matrix)
    plus = [values[l] + values[7 - l] for l in range(HALF)]
    minus = [values[l] - values[7 - l] for l in range(HALF)]
    result = [None] * QUAD_POINT_TALLY
    for i in range(HALF):
        from_plus = sum(float(even[i, l]) * plus[l] for l in range(HALF))
        from_minus = sum(float(odd[i, l]) * minus[l] for l in range(HALF))
        result[i] = from_plus + from_minus
        result[7 - i] = from_plus - from_minus
    return result


def stacked_matrix(matrix):
    whole = matrix.astype(np.float32)
    high = whole.astype(jnp.bfloat16)
    low = (whole - high.astype(np.float32)).astype(jnp.bfloat16)
    return np.concatenate([high, low, high], axis=1)


def height_product(stacked, values):
    high = values.astype(jnp.bfloat16)
    low = (values - high.astype(jnp.float32)).astype(jnp.bfloat16)
    both = jnp.concatenate([high, high, low], axis=0)
    return jnp.dot(stacked, both, preferred_element_type=jnp.float32)


def rows_of(j):
    return slice(QUAD_POINT_TALLY * j, QUAD_POINT_TALLY * (j + 1))


def height_weights(shape):
    level = lax.broadcasted_iota(jnp.int32, shape, 0)
    result = jnp.full(shape, float(WEIGHTS[0]), jnp.float32)
    for k in range(1, QUAD_POINT_TALLY):
        result = jnp.where(level == k, float(WEIGHTS[k]), result)
    return result


def copy_weights(shape):
    level = lax.broadcasted_iota(jnp.int32, shape, 0)
    layer = lax.broadcasted_iota(jnp.int32, shape, 1)
    shared = ((level == 0) & (layer > 0)) | (
        (level == QUAD_POINT_TALLY - 1) & (layer < shape[1] - 1)
    )
    return jnp.where(shared, 0.5, 1.0)


def side_weight(i, j):
    return (0.5 if i in (0, 7) else 1.0) * (0.5 if j in (0, 7) else 1.0)


HEIGHT, SIDE, HEIGHT_BACK, HEIGHT_SQUARE = (slice(n * ROWS, (n + 1) * ROWS) for n in range(4))
BOTH = slice(0, 2 * ROWS)


def constants():
    one = np.eye(QUAD_POINT_TALLY)
    return jnp.asarray(
        np.concatenate([
            stacked_matrix(np.kron(one, DERIV)),
            stacked_matrix(np.kron(DERIV, one)),
            stacked_matrix(np.kron(one, DERIV.T)),
            stacked_matrix(np.kron(one, (DERIV * DERIV).T)),
        ])
    )


def dom_sides():
    odd = lax.rem(lax.axis_index("dom"), 2)
    return 7 * (1 - odd), 7 * odd


def batch_sides():
    odd = lax.rem(lax.axis_index("batch"), 2)
    return 1 - odd, odd


UPPER = pl.ds(QUAD_POINT_TALLY - 1, QUAD_POINT_TALLY, stride=QUAD_POINT_TALLY)
LOWER = pl.ds(0, QUAD_POINT_TALLY, stride=QUAD_POINT_TALLY)
TAIL = slice(LAST, ROWS)
HEAD = slice(0, QUAD_POINT_TALLY)


def sum_heights(field, slot):
    layers = field.shape[3]
    lane = lax.broadcasted_iota(jnp.int32, (QUAD_POINT_TALLY, layers), 1)
    for i in range(field.shape[0]):
        upper = field[i, slot, UPPER, :]
        lower = field[i, slot, LOWER, :]
        above = jnp.where(lane < layers - 1, pltpu.roll(lower, layers - 1, 1), 0.0)
        below = jnp.where(lane > 0, pltpu.roll(upper, 1, 1), 0.0)
        field[i, slot, UPPER, :] = upper + above
        field[i, slot, LOWER, :] = lower + below


def face_rows(b):
    return slice(b * LAST, b * LAST + ROWS)


class Parts:
    def __init__(self, inner, ends):
        self.inner, self.ends = inner, ends
        self.blocks = inner.shape[1] + 2

    def at(self, b):
        if b in (0, self.blocks - 1):
            return self.ends, min(b, 1)
        return self.inner, b - 1

    def load(self, i, b, rows):
        field, slot = self.at(b)
        return field[i, slot, rows, :]


class Whole:
    def __init__(self, field):
        self.field, self.blocks = field, field.shape[1]

    def load(self, i, b, rows):
        return self.field[i, b, rows, :]


def joined(parts, i, b, out):
    out[...] = parts.load(i, b, slice(0, ROWS))
    if b > 0:
        out[HEAD, :] = out[HEAD, :] + parts.load(i, b - 1, TAIL)
    if b < parts.blocks - 1:
        out[TAIL, :] = out[TAIL, :] + parts.load(i, b + 1, HEAD)


def emit_faces(parts, first, second, corner, n=0):
    for side, face in zip(dom_sides(), (first, second)):
        for b in range(parts.blocks):
            joined(parts, side, b, face.at[n, face_rows(b)])
    _, side = dom_sides()
    corner[n, rows_of(0), :] = parts.load(side, 0, HEAD)
    corner[n, rows_of(1), :] = parts.load(side, parts.blocks - 1, TAIL)


def emit_ends(parts, ends):
    for i in range(QUAD_POINT_TALLY):
        ends[0, i] = parts.load(i, 0, HEAD)
        ends[1, i] = parts.load(i, parts.blocks - 1, TAIL)


def assemble(parts, b, out, slot, dom_received, batch_received):
    for i in range(QUAD_POINT_TALLY):
        joined(parts, i, b, out.at[i, slot])
    for side, received in zip(dom_sides(), dom_received):
        out[side, slot] = out[side, slot] + received[face_rows(b), :]
    if batch_received is not None and b in (0, parts.blocks - 1):
        rows = HEAD if b == 0 else TAIL
        low, _ = batch_sides()
        from_first = low == (0 if b == 0 else 1)
        for i in range(QUAD_POINT_TALLY):
            received = jnp.where(from_first, batch_received[0][i], batch_received[1][i])
            out[i, slot, rows, :] = out[i, slot, rows, :] + received


def clear_top(field, slot, keep, b):
    for i in range(QUAD_POINT_TALLY):
        field[i, slot, UPPER, :] = field[i, slot, UPPER, :] * keep[i, b]


def apply_block(field, slot, metric, b, scratch_s, scratch_t, out, matrices, scale=1.0, extra=None):
    both, height_back = matrices[BOTH], matrices[HEIGHT_BACK]
    back = DERIV.T
    for i in range(QUAD_POINT_TALLY):
        slopes = height_product(both, field[i, slot])
        scratch_t[i] = slopes[:ROWS]
        scratch_s[i] = slopes[ROWS:]
    for j in range(QUAD_POINT_TALLY):
        rows = rows_of(j)
        along_r = deriv_line(DERIV, [field[i, slot, rows, :] for i in range(QUAD_POINT_TALLY)])
        flux_r = []
        additions = []
        for i in range(QUAD_POINT_TALLY):
            along_s, along_t = scratch_s[i, rows, :], scratch_t[i, rows, :]
            rr, ss, tt = (metric[n, i, b, rows, :] for n in range(3))
            rs, rt, st = (metric[n, i, b, rows, :] for n in range(3, 6))
            flux_r.append(rr * along_r[i] + rs * along_s + rt * along_t)
            scratch_s[i, rows, :] = rs * along_r[i] + ss * along_s + st * along_t
            scratch_t[i, rows, :] = rt * along_r[i] + st * along_s + tt * along_t
            if extra is not None:
                additions.append(extra(i, j, along_r[i], along_s, along_t))
        result = deriv_line(scale * back, flux_r)
        for i in range(QUAD_POINT_TALLY):
            out[i, slot, rows, :] = result[i] if extra is None else result[i] + additions[i]
    total = None
    for i in range(QUAD_POINT_TALLY):
        block = scratch_s[i]
        from_s = deriv_line(scale * back, [block[rows_of(j)] for j in range(QUAD_POINT_TALLY)])
        from_t = height_product(height_back, scratch_t[i])
        for j in range(QUAD_POINT_TALLY):
            rows = rows_of(j)
            term = from_t[rows] if scale == 1.0 else scale * from_t[rows]
            value = out[i, slot, rows, :] + from_s[j] + term
            out[i, slot, rows, :] = value
            if extra is None:
                term = field[i, slot, rows, :] * value
                total = term if total is None else total + term
    return total


def dot_weighted(left, right, slot):
    layers = left.shape[3]
    sums = {}
    for i in range(QUAD_POINT_TALLY):
        for j in range(QUAD_POINT_TALLY):
            weight = side_weight(i, j)
            term = left[i, slot, rows_of(j), :] * right[i, slot, rows_of(j), :]
            sums[weight] = sums[weight] + term if weight in sums else term
    total = sums[1.0] + 0.5 * sums[0.5] + 0.25 * sums[0.25]
    return total * copy_weights((QUAD_POINT_TALLY, layers))


def mass_faces_kernel(
    determinant, prior, first, second, corner, ends, prior_ends, sides, planes, det_face, det_end, prior_face, prior_end,
    mass_face, mass_end, sems,
):
    blocks, layers = determinant.shape[1], first.shape[2]
    last = blocks - 1
    copies = []
    for n, i in enumerate((0, 7)):
        copies.append((determinant.at[i], det_face.at[n]))
        copies.append((prior.at[i], prior_face.at[n]))
    for n, (b, j) in enumerate(((0, 0), (last, 7))):
        copies.append((determinant.at[:, b, j], det_end.at[n]))
        copies.append((prior.at[:, b, j], prior_end.at[n]))
    started = [
        pltpu.make_async_copy(source, target, sems.at[n])
        for n, (source, target) in enumerate(copies)
    ]
    for copy in started:
        copy.start()
    for copy in started:
        copy.wait()
    weights = height_weights((QUAD_POINT_TALLY, layers))
    tile = (QUAD_POINT_TALLY, layers)
    for n, (end, plane) in enumerate(zip(batch_sides(), dom_sides())):
        sides[n] = jnp.full(tile, end.astype(jnp.float32))
        for i in range(QUAD_POINT_TALLY):
            planes[n, i] = jnp.full(tile, (plane == i).astype(jnp.float32))
    for n, i in enumerate((0, 7)):
        for b in range(blocks):
            for j in range(QUAD_POINT_TALLY):
                weight = weights * float(WEIGHTS[i] * WEIGHTS[j])
                value = weight * det_face[n, b, j].astype(jnp.float32)
                mass_face[0, n, b, rows_of(j), :] = value
                mass_face[1, n, b, rows_of(j), :] = value * prior_face[n, b, j]
    for side, j in enumerate((0, 7)):
        for i in range(QUAD_POINT_TALLY):
            weight = weights * float(WEIGHTS[i] * WEIGHTS[j])
            value = weight * det_end[side, i].astype(jnp.float32)
            mass_end[0, 0, side, rows_of(i), :] = value
            mass_end[1, 0, side, rows_of(i), :] = value * prior_end[side, i]
    for n in range(2):
        for b in range(blocks):
            sum_heights(mass_face.at[n], b)
        for side in range(2):
            sum_heights(mass_end.at[n], side)
            for i in range(QUAD_POINT_TALLY):
                (ends, prior_ends)[n][0, side, i] = mass_end[n, 0, side, rows_of(i), :]
        for b in range(blocks - 1):
            for face in range(2):
                total = mass_face[n, face, b, TAIL, :] + mass_face[n, face, b + 1, HEAD, :]
                mass_face[n, face, b, TAIL, :] = total
                mass_face[n, face, b + 1, HEAD, :] = total
        odd, _ = dom_sides()
        face_first = jnp.minimum(odd, 1)
        for b in range(blocks):
            first[n, face_rows(b), :] = mass_face[n, face_first, b]
            second[n, face_rows(b), :] = mass_face[n, 1 - face_first, b]
        corner[n, rows_of(0), :] = mass_face[n, 1 - face_first, 0, HEAD, :]
        corner[n, rows_of(1), :] = mass_face[n, 1 - face_first, last, TAIL, :]


def prepare_kernel(
    determinant, prior, pure, mixed, matrices, mass, mass_prior, metric, diagonal,
    det_in, prior_in, pure_in, mixed_in, sems,
):
    blocks, layers = diagonal.shape[1], diagonal.shape[3]
    weights = height_weights((QUAD_POINT_TALLY, layers))
    level = lax.broadcasted_iota(jnp.int32, (QUAD_POINT_TALLY, layers), 0)
    ends = [float(DERIV[i, i]) for i in range(QUAD_POINT_TALLY)]
    height_ends = jnp.where(level == 0, ends[0], jnp.where(level == 7, ends[7], 0.0))
    squares = DERIV * DERIV

    def mass_copies(b):
        return (
            pltpu.make_async_copy(determinant.at[:, b], det_in.at[:, b], sems.at[0, b]),
            pltpu.make_async_copy(prior.at[:, b], prior_in.at[:, b], sems.at[1, b]),
        )

    def metric_copies(b):
        return (
            pltpu.make_async_copy(pure.at[:, :, b], pure_in.at[:, :, b], sems.at[2, b]),
            pltpu.make_async_copy(mixed.at[:, :, b], mixed_in.at[:, :, b], sems.at[3, b]),
        )

    for copies in (mass_copies, metric_copies):
        for b in range(blocks):
            for copy in copies(b):
                copy.start()

    def mass_block(b, carry):
        for copy in mass_copies(b):
            copy.wait()
        for i in range(QUAD_POINT_TALLY):
            for j in range(QUAD_POINT_TALLY):
                weight = weights * float(WEIGHTS[i] * WEIGHTS[j])
                value = weight * det_in[i, b, j].astype(jnp.float32)
                mass[i, b, rows_of(j), :] = value
                mass_prior[i, b, rows_of(j), :] = value * prior_in[i, b, j]
        sum_heights(mass, b)
        sum_heights(mass_prior, b)
        return carry

    def metric_block(b, carry):
        for copy in metric_copies(b):
            copy.wait()
        for i in range(QUAD_POINT_TALLY):
            for j in range(QUAD_POINT_TALLY):
                weight = weights * float(WEIGHTS[i] * WEIGHTS[j])
                for n in range(3):
                    metric[n, i, b, rows_of(j), :] = weight * pure_in[n, i, b, j].astype(
                        jnp.float32
                    )
                    metric[n + 3, i, b, rows_of(j), :] = weight * mixed_in[n, i, b, j].astype(
                        jnp.float32
                    )
        for j in range(QUAD_POINT_TALLY):
            line = square_line(
                squares.T, [metric[0, i, b, rows_of(j), :] for i in range(QUAD_POINT_TALLY)]
            )
            for i in range(QUAD_POINT_TALLY):
                diagonal[i, b, rows_of(j), :] = line[i]
        for i in range(QUAD_POINT_TALLY):
            line = square_line(
                squares.T, [metric[1, i, b, rows_of(j), :] for j in range(QUAD_POINT_TALLY)]
            )
            from_t = height_product(matrices[HEIGHT_SQUARE], metric[2, i, b])
            for j in range(QUAD_POINT_TALLY):
                rows = rows_of(j)
                value = diagonal[i, b, rows, :] + line[j] + from_t[rows]
                if ends[i] != 0.0 and ends[j] != 0.0:
                    value = value + (2.0 * ends[i] * ends[j]) * metric[3, i, b, rows, :]
                if ends[i] != 0.0:
                    value = value + (2.0 * ends[i]) * height_ends * metric[4, i, b, rows, :]
                if ends[j] != 0.0:
                    value = value + (2.0 * ends[j]) * height_ends * metric[5, i, b, rows, :]
                diagonal[i, b, rows, :] = value
        sum_heights(diagonal, b)
        return carry

    lax.fori_loop(0, blocks, mass_block, 0)
    lax.fori_loop(0, blocks, metric_block, 0)


def source_kernel(
    metric, heat, wind, determinant, diagonal, matrices,
    numerator, first, second, corner, diag_ends, heat_ends, scratch_s, scratch_t,
):
    blocks, layers = numerator.shape[1], numerator.shape[3]
    weights = height_weights((QUAD_POINT_TALLY, layers))

    def block(b, carry):
        def extra(i, j, along_r, along_s, along_t):
            weight = weights * float(WEIGHTS[i] * WEIGHTS[j])
            convection = (
                wind[0, i, b, j].astype(jnp.float32) * along_r
                + wind[1, i, b, j].astype(jnp.float32) * along_s
                + wind[2, i, b, j].astype(jnp.float32) * along_t
            )
            return weight * (
                determinant[i, b, j].astype(jnp.float32) * heat[i, b, rows_of(j), :]
                - transport_increment * convection
            )

        apply_block(
            heat, b, metric, b, scratch_s, scratch_t, numerator, matrices,
            -conduction_increment, extra,
        )
        sum_heights(numerator, b)
        return carry

    lax.fori_loop(0, blocks, block, 0)
    for n, (field, ends) in enumerate(((diagonal, diag_ends), (numerator, heat_ends))):
        emit_faces(Whole(field), first, second, corner, n)
        emit_ends(Whole(field), ends.at[0])


def ends_kernel(offsets, *refs):
    inputs, (first, second) = refs[: 3 * len(offsets)], refs[3 * len(offsets) :]
    for n, offset in enumerate(offsets):
        ends, *received = inputs[3 * n : 3 * n + 3]
        lasts = [face.shape[1] - QUAD_POINT_TALLY for face in received]
        for side, target in zip(batch_sides(), (first, second)):
            for i in range(QUAD_POINT_TALLY):
                target[n, i] = ends[0, side, i]
            for dom_side, face, last in zip(dom_sides(), received, lasts):
                rows = pl.ds(pl.multiple_of(side * last, QUAD_POINT_TALLY), QUAD_POINT_TALLY)
                target[n, dom_side] = target[n, dom_side] + face[offset, rows, :]


def elements(inner, blocks):
    return list(enumerate(range(1, blocks - 1) if inner else (0, blocks - 1)))


class Sending:
    def __init__(self, sems):
        self.sems, self.copies = sems, []

    def start(self, source, target):
        copy = pltpu.make_async_copy(source, target, self.sems.at[len(self.copies)])
        copy.start()
        self.copies.append(copy)

    def wait(self):
        for copy in self.copies:
            copy.wait()


def start_source(determinant, spread, b):
    layers = spread.shape[3]
    weights = height_weights((QUAD_POINT_TALLY, layers))

    def extra(i, j, along_r, along_s, along_t):
        weight = weights * float(-WEIGHTS[i] * WEIGHTS[j] / step_dt)
        return (weight * determinant[i, b, j].astype(jnp.float32)) * spread[i, b, rows_of(j), :]

    return extra


def assemble_head(mass, mass_prior, dom, batch, keep, slot, b, mass_inverse, head):
    for n, (field, out) in enumerate(((mass, mass_inverse), (mass_prior, head))):
        assemble(
            Whole(field), b, out, slot, tuple(face.at[n] for face in dom),
            batch and tuple(face.at[n] for face in batch),
        )
    clear_top(head, slot, keep, b)
    for i in range(QUAD_POINT_TALLY):
        inverse = 1.0 / mass_inverse[i, slot]
        mass_inverse[i, slot] = inverse
        head[i, slot] = head[i, slot] * inverse


def start_inner_kernel(
    mass, mass_prior, dom_first, dom_second, metric, spread, determinant, keep, matrices,
    head_out, mass_inverse, residual, scratch_s, scratch_t, head, sems,
):
    blocks = mass.shape[1]
    sending = Sending(sems)
    for slot, b in elements(True, blocks):
        assemble_head(
            mass, mass_prior, (dom_first, dom_second), None, keep, slot, b, mass_inverse, head
        )
        sending.start(head.at[:, slot], head_out.at[:, slot])
        apply_block(
            head, slot, metric, b, scratch_s, scratch_t, residual, matrices, -1.0,
            start_source(determinant, spread, b),
        )
        sum_heights(residual, slot)
    sending.wait()


def start_ends_kernel(
    mass, mass_prior, dom_first, dom_second, batch_first, batch_second,
    metric, spread, determinant, keep, matrices, residual_inner,
    head_out, mass_inverse, residual, first, second, corner, ends,
    scratch_s, scratch_t, head, sems,
):
    blocks = mass.shape[1]
    sending = Sending(sems)
    for slot, b in elements(False, blocks):
        assemble_head(
            mass, mass_prior, (dom_first, dom_second), (batch_first, batch_second), keep,
            slot, b, mass_inverse, head,
        )
        sending.start(head.at[:, slot], head_out.at[:, slot])
        apply_block(
            head, slot, metric, b, scratch_s, scratch_t, residual, matrices, -1.0,
            start_source(determinant, spread, b),
        )
        sum_heights(residual, slot)
    parts = Parts(residual_inner, residual)
    emit_faces(parts, first, second, corner)
    emit_ends(parts, ends.at[0])
    sending.wait()


def row_sums(*parts):
    rows = [jnp.sum(part, axis=0, keepdims=True) for part in parts]
    rows.append(jnp.zeros((QUAD_POINT_TALLY - len(parts), parts[0].shape[1]), jnp.float32))
    return jnp.concatenate(rows, axis=0)


def assemble_direction(
    residual_parts, diagonal, res_dom, diag_dom, batch, keep, slot, b,
    residual, diag_inverse, direction,
):
    assemble(
        residual_parts, b, residual, slot, tuple(face.at[0] for face in res_dom),
        batch and tuple(face.at[0] for face in batch),
    )
    assemble(
        Whole(diagonal), b, diag_inverse, slot, tuple(face.at[0] for face in diag_dom),
        batch and tuple(face.at[1] for face in batch),
    )
    clear_top(residual, slot, keep, b)
    for i in range(QUAD_POINT_TALLY):
        inverse = 1.0 / diag_inverse[i, slot]
        diag_inverse[i, slot] = inverse
        direction[i, slot] = residual[i, slot] * inverse


def apply_dots(left, field, inner, metric, scratch_s, scratch_t, out, matrices):
    energy = product = 0.0
    for slot, b in elements(inner, metric.shape[2]):
        energy += apply_block(field, slot, metric, b, scratch_s, scratch_t, out, matrices)
        product += dot_weighted(left, field, slot)
        sum_heights(out, slot)
    return product, energy


def first_inner_kernel(
    residual_inner, residual_ends, diagonal, res_first, res_second, diag_first, diag_second,
    metric, keep, matrices,
    direction_out, diag_inverse, image, dots, scratch_s, scratch_t, residual, direction, sems,
):
    sending = Sending(sems)
    for slot, b in elements(True, diagonal.shape[1]):
        assemble_direction(
            Parts(residual_inner, residual_ends), diagonal, (res_first, res_second),
            (diag_first, diag_second), None, keep, slot, b, residual, diag_inverse, direction,
        )
        sending.start(direction.at[:, slot], direction_out.at[:, slot])
    dots[...] = row_sums(
        *apply_dots(residual, direction, True, metric, scratch_s, scratch_t, image, matrices)
    )
    sending.wait()


def first_ends_kernel(
    residual_inner, residual_ends, diagonal, res_first, res_second, diag_first, diag_second,
    batch_first, batch_second, metric, keep, matrices, image_inner, dots_inner,
    direction_out, diag_inverse, image, first, second, corner, ends, dots,
    scratch_s, scratch_t, residual, direction, sems,
):
    sending = Sending(sems)
    for slot, b in elements(False, diagonal.shape[1]):
        assemble_direction(
            Parts(residual_inner, residual_ends), diagonal, (res_first, res_second),
            (diag_first, diag_second), (batch_first, batch_second), keep, slot, b,
            residual, diag_inverse, direction,
        )
        sending.start(direction.at[:, slot], direction_out.at[:, slot])
    dots[...] = dots_inner[...] + row_sums(
        *apply_dots(residual, direction, False, metric, scratch_s, scratch_t, image, matrices)
    )
    parts = Parts(image_inner, image)
    emit_faces(parts, first, second, corner)
    emit_ends(parts, ends.at[0])
    sending.wait()


def second_inner_kernel(
    image_inner, image_ends, dom_first, dom_second, diag_inverse, metric, keep, matrices, dots_in,
    scaled_out, image_two, dots, scratch_s, scratch_t, image, scaled, sems,
):
    parts = Parts(image_inner, image_ends)
    sending = Sending(sems)
    for slot, b in elements(True, parts.blocks):
        assemble(parts, b, image, slot, (dom_first.at[0], dom_second.at[0]), None)
        clear_top(image, slot, keep, b)
        for i in range(QUAD_POINT_TALLY):
            scaled[i, slot] = image[i, slot] * diag_inverse[i, slot]
        sending.start(scaled.at[:, slot], scaled_out.at[:, slot])
    product, energy = apply_dots(
        image, scaled, True, metric, scratch_s, scratch_t, image_two, matrices
    )
    nothing = jnp.zeros_like(energy)
    dots[...] = dots_in[...] + row_sums(nothing, nothing, product, energy)
    sending.wait()


def second_ends_kernel(
    image_inner, image_ends, dom_first, dom_second, batch_first, batch_second,
    diag_inverse, metric, keep, matrices, two_inner, dots_in,
    scaled_out, image_two, first, second, corner, ends, all_dots,
    scratch_s, scratch_t, image, scaled, sems,
):
    parts = Parts(image_inner, image_ends)
    sending = Sending(sems)
    for slot, b in elements(False, parts.blocks):
        assemble(
            parts, b, image, slot, (dom_first.at[0], dom_second.at[0]),
            (batch_first.at[0], batch_second.at[0]),
        )
        clear_top(image, slot, keep, b)
        for i in range(QUAD_POINT_TALLY):
            scaled[i, slot] = image[i, slot] * diag_inverse[i, slot]
        sending.start(scaled.at[:, slot], scaled_out.at[:, slot])
    product, energy = apply_dots(
        image, scaled, False, metric, scratch_s, scratch_t, image_two, matrices
    )
    nothing = jnp.zeros_like(energy)
    sums = dots_in[...] + row_sums(nothing, nothing, product, energy)
    for n in range(all_dots.shape[0]):
        all_dots[n] = sums
    parts = Parts(two_inner, image_two)
    emit_faces(parts, first, second, corner)
    emit_ends(parts, ends.at[0])
    sending.wait()


def heat_kernel(
    numerator, dom_first, dom_second, inverse_inner, inverse_ends, heat, values, factors
):
    blocks = heat.shape[1]
    inverse = Parts(inverse_inner, inverse_ends)
    for b in range(blocks):
        assemble(Whole(numerator), b, heat, b, (dom_first.at[1], dom_second.at[1]), None)
        for i in range(QUAD_POINT_TALLY):
            heat[i, b] = heat[i, b] * inverse.load(i, b, slice(0, ROWS))
    for side, (b, rows) in enumerate(((0, HEAD), (blocks - 1, TAIL))):
        for i in range(QUAD_POINT_TALLY):
            values[side, i] = heat[i, b, rows, :]
            factors[side, i] = inverse.load(i, b, rows)


CHUNK = 1


def last_kernel(
    image_inner, image_ends, dom_first, dom_second, diag_inner, diag_ends, keep, all_dots,
    head_inner, head_ends, direction_inner, direction_ends, scaled_inner, scaled_ends,
    out_head, out_defect, end_values, end_factors,
    image, far, result_head, result_defect, sems_in, sems_out,
):
    sources = (
        head_inner, head_ends, direction_inner, direction_ends, scaled_inner, scaled_ends
    )
    chunks = QUAD_POINT_TALLY // CHUNK
    arriving = []
    for c in range(chunks):
        planes = pl.ds(c * CHUNK, CHUNK)
        arriving.append([
            pltpu.make_async_copy(
                source.at[planes], far.at[n // 2, n % 2, planes], sems_in.at[c, n]
            )
            for n, source in enumerate(sources)
        ])
        for copy in arriving[-1]:
            copy.start()
    parts, inverses = Parts(image_inner, image_ends), Parts(diag_inner, diag_ends)
    blocks, layers = parts.blocks, image.shape[3]
    level = lax.broadcasted_iota(jnp.int32, (QUAD_POINT_TALLY, layers), 0)
    sums = all_dots[0]
    for n in range(1, all_dots.shape[0]):
        sums = sums + all_dots[n]
    sums = jnp.sum(sums, axis=1, keepdims=True)
    inner, energy, cross, energy_two = (sums[n : n + 1] for n in range(4))
    step = inner / energy
    following = step * step * cross - inner
    growth = 1.0 + following / inner
    curvature = growth * growth * energy - 2.0 * growth * step * cross + step * step * energy_two
    step_two = following / curvature
    along_direction = step + step_two * growth
    along_scaled = step * step_two
    whole = slice(0, ROWS)
    for b in range(blocks):
        for i in range(QUAD_POINT_TALLY):
            joined(parts, i, b, image.at[i, b])
        for side, received in zip(dom_sides(), (dom_first, dom_second)):
            image[side, b] = image[side, b] + received[0, face_rows(b), :]
        clear_top(image, b, keep, b)
    leaving = []
    for c in range(chunks):
        planes = pl.ds(c * CHUNK, CHUNK)
        for copy in arriving[c]:
            copy.wait()
        for i in range(c * CHUNK, (c + 1) * CHUNK):
            for b in range(blocks):
                kind, slot = (1, min(b, 1)) if b in (0, blocks - 1) else (0, b - 1)
                start, change = far[1, kind, i, slot], far[2, kind, i, slot]
                inverse = inverses.load(i, b, whole)
                result_head[i, b] = (
                    far[0, kind, i, slot] + along_direction * start - along_scaled * change
                )
                result_defect[i, b] = (
                    start - along_direction * change + along_scaled * (image[i, b] * inverse)
                )
            for side, (b, j) in enumerate(((0, 0), (blocks - 1, 7))):
                end_values[side, i] = result_defect[i, b, rows_of(j), :]
                top = jnp.where(level == 7, keep[i, b, j : j + 1, :], 1.0)
                end_factors[side, i] = along_scaled * top * inverses.load(i, b, rows_of(j))
        for n, (source, target) in enumerate(
            ((result_head, out_head), (result_defect, out_defect))
        ):
            copy = pltpu.make_async_copy(source.at[planes], target.at[planes], sems_out.at[c, n])
            copy.start()
            leaving.append(copy)
    for copy in leaving:
        copy.wait()


def close_kernel(
    defect, heat, batch_first, batch_second, defect_values, defect_factors, heat_values,
    heat_factors, out_defect, out_heat, rows, sems,
):
    del defect, heat
    low, _ = batch_sides()
    copies = []
    for n, (values, factors, out) in enumerate((
        (defect_values, defect_factors, out_defect), (heat_values, heat_factors, out_heat)
    )):
        for side, (b, start) in enumerate(((0, 0), (out.shape[1] - 1, LAST))):
            for i in range(QUAD_POINT_TALLY):
                received = jnp.where(low == side, batch_first[n, i], batch_second[n, i])
                rows[n, side, i] = values[side, i] + factors[side, i] * received
            copy = pltpu.make_async_copy(
                rows.at[n, side], out.at[:, b, pl.ds(start, QUAD_POINT_TALLY), :],
                sems.at[n, side],
            )
            copy.start()
            copies.append(copy)
    for copy in copies:
        copy.wait()


COST = {
    "mass_faces": 2, "prepare": 10, "source": 14, "start_inner": 8, "start_faces": 4,
    "start_ends": 8, "first_inner": 8, "first_faces": 4, "first_ends": 6, "heat": 4,
    "second_inner": 8, "second_ends": 8, "last": 12, "close": 2,
}


def call(kernel, name, outs, args, scratch=(), far_in=(), far_out=(), aliases=None):
    near, far = pl.BlockSpec(memory_space=pltpu.VMEM), pl.BlockSpec(memory_space=pltpu.HBM)
    args = [
        pltpu.with_memory_space_constraint(arg, pltpu.HBM) if n in far_in else arg
        for n, arg in enumerate(args)
    ]
    return pl.pallas_call(
        kernel,
        name=name,
        out_shape=[
            (pltpu.HBM if n in far_out else jax.ShapeDtypeStruct)(shape, jnp.float32)
            for n, shape in enumerate(outs)
        ],
        in_specs=[far if n in far_in else near for n in range(len(args))],
        out_specs=[far if n in far_out else near for n in range(len(outs))],
        scratch_shapes=[
            shape if not isinstance(shape, tuple) else pltpu.VMEM(shape, jnp.float32)
            for shape in scratch
        ],
        input_output_aliases=aliases or {},
        cost_estimate=pl.CostEstimate(
            flops=0, bytes_accessed=COST.get(name, 0) * 1000000, transcendentals=0
        ),
        compiler_params=pltpu.CompilerParams(vmem_limit_bytes=VMEM_LIMIT),
    )(*args)


def near_swap(array, axis):
    count = lax.axis_size(axis)
    return lax.ppermute(array, axis, [(index, index ^ 1) for index in range(count)])


def far_swap(array, axis):
    count = lax.axis_size(axis)
    pairs = [(index, (((index + 1) ^ 1) - 1) % count) for index in range(count)]
    return lax.ppermute(array, axis, pairs)


def swaps(first, second, axis):
    return near_swap(first, axis), far_swap(second, axis)


def shards(
    heat_state_element,
    wind_reference_flux,
    geometric_pure_factors,
    geometric_mixed_factors,
    mapping_determinant,
    velocity_source_spread,
    prior_head_state,
    exit_boundary_marks,
):
    _, points, blocks, _, _, layers = heat_state_element.shape
    block_shape = (points, blocks, ROWS, layers)
    inner_shape = (points, blocks - 2, ROWS, layers)
    ends_shape = (points, 2, ROWS, layers)
    heat = heat_state_element.reshape(block_shape)
    spread = velocity_source_spread.reshape(block_shape)
    prior = prior_head_state[0]
    wind, pure, mixed = (
        array.reshape(array.shape[:1] + array.shape[2:])
        for array in (wind_reference_flux, geometric_pure_factors, geometric_mixed_factors)
    )
    determinant = mapping_determinant[0]
    layer = lax.broadcasted_iota(jnp.int32, (points, blocks, points, layers), 3)
    marks = exit_boundary_marks[0].astype(jnp.float32)[:, :, :, None]
    keep = jnp.where(layer == layers - 1, 1.0 - marks, 1.0)
    matrices = constants()

    end_shape = (1, 2, points, points, layers)

    def faces(count):
        face = (count, blocks * LAST + QUAD_POINT_TALLY, layers)
        return [face] * 2 + [(count, 2 * QUAD_POINT_TALLY, layers)]

    def dom_swaps(first, second, corner):
        corner = far_swap(corner, "dom")
        near = near_swap(first, "dom")
        return (near, far_swap(second, "dom")), (near, corner)

    def ends_call(*groups):
        results = []
        for side in range(2):
            high = sides[side] > 0.0
            fields = []
            for ends, *received, place in groups:
                field = jnp.where(high[None], ends[0, 1], ends[0, 0])
                for plane_mask, face in zip(planes, received):
                    tail = face[place, face.shape[1] - points :]
                    rows = jnp.where(high, tail, face[place, :points])
                    field = field + plane_mask * rows[None]
                fields.append(field)
            results.append(jnp.stack(fields))
        return results

    def mass_call(ends, *received):
        return call(
            functools.partial(ends_kernel, (0, 1)), "mass_ends",
            [(2, points, points, layers)] * 2, [ends[0], *received, ends[1], *received],
        )

    pair = [(points, ROWS, layers)] * 2
    plane = (points, layers)

    *mass_faces, mass_end, prior_end, sides, planes = call(
        mass_faces_kernel, "mass_faces",
        faces(2) + [end_shape] * 2 + [(2,) + plane, (2, points) + plane], [determinant, prior],
        [
            pltpu.VMEM((2, blocks, points, points, layers), jnp.bfloat16),
            pltpu.VMEM((2, points, points, layers), jnp.bfloat16),
            (2, blocks, points, points, layers),
            (2, points, points, layers),
            (2, 2, blocks, ROWS, layers),
            (2, 1, 2, ROWS, layers),
            pltpu.SemaphoreType.DMA((8,)),
        ],
        far_in=(0, 1),
    )
    mass_dom = swaps(*mass_faces[:2], "dom")
    mass, mass_prior, metric, diagonal = call(
        prepare_kernel, "prepare", [block_shape] * 2 + [(6,) + block_shape, block_shape],
        [determinant, prior, pure, mixed, matrices],
        [
            pltpu.VMEM(determinant.shape, jnp.bfloat16),
            prior.shape,
            pltpu.VMEM(pure.shape, jnp.bfloat16),
            pltpu.VMEM(mixed.shape, jnp.bfloat16),
            pltpu.SemaphoreType.DMA((4, blocks)),
        ],
        far_in=range(4),
    )
    numerator, *source_faces, diag_end, heat_end = call(
        source_kernel, "source", [block_shape] + faces(2) + [end_shape] * 2,
        [metric, heat, wind, determinant, diagonal, matrices], pair,
    )
    source_dom = swaps(*source_faces[:2], "dom")
    mass_batch = swaps(
        *mass_call((mass_end, prior_end), *mass_dom), "batch"
    )
    sems = pltpu.SemaphoreType.DMA
    common = [metric, spread, determinant]
    head_inner, inverse_inner, residual_inner = call(
        start_inner_kernel, "start_inner", [inner_shape] * 3,
        [mass, mass_prior, *mass_dom, *common, keep, matrices],
        pair + [inner_shape, sems((blocks,))], far_out=(0,),
    )
    head_ends, inverse_ends, residual_ends, *res_faces, res_end = call(
        start_ends_kernel, "start_ends", [ends_shape] * 3 + faces(1) + [end_shape],
        [mass, mass_prior, *mass_dom, *mass_batch, *common, keep, matrices, residual_inner],
        pair + [ends_shape, sems((2,))], far_out=(0,),
    )
    res_dom, res_corners = dom_swaps(*res_faces)
    res_batch = swaps(
        *ends_call((res_end, *res_corners, 0), (diag_end, *source_dom, 0)),
        "batch",
    )
    residual = [residual_inner, residual_ends, diagonal, *res_dom, *source_dom]
    direction_inner, diag_inner, image_inner, dots_inner = call(
        first_inner_kernel, "first_inner", [inner_shape] * 3 + [plane],
        [*residual, metric, keep, matrices], pair + [inner_shape] * 2 + [sems((blocks,))],
        far_out=(0,),
    )
    direction_ends, diag_ends, image_ends, *image_faces, image_end, dots = call(
        first_ends_kernel, "first_ends", [ends_shape] * 3 + faces(1) + [end_shape, plane],
        [*residual, *res_batch, metric, keep, matrices, image_inner, dots_inner],
        pair + [ends_shape] * 2 + [sems((2,))], far_out=(0,),
    )
    image_dom, image_corners = dom_swaps(*image_faces)
    heat_next, heat_values, heat_factors = call(
        heat_kernel, "heat", [block_shape] + [(2, points) + plane] * 2,
        [numerator, *source_dom, inverse_inner, inverse_ends],
    )
    image_batch = swaps(*ends_call((image_end, *image_corners, 0)), "batch")
    heat_next, received = lax.optimization_barrier((heat_next, image_batch[0]))
    image_batch = (received, image_batch[1])
    count = lax.axis_size("dom") * lax.axis_size("batch")
    image = [image_inner, image_ends, *image_dom]
    scaled_inner, two_inner, dots = call(
        second_inner_kernel, "second_inner", [inner_shape] * 2 + [plane],
        [*image, diag_inner, metric, keep, matrices, dots],
        pair + [inner_shape] * 2 + [sems((blocks,))], far_out=(0,),
    )
    scaled_ends, two_ends, *two_faces, two_end, all_dots = call(
        second_ends_kernel, "second_ends",
        [ends_shape] * 2 + faces(1) + [end_shape, (count,) + plane],
        [*image, *image_batch, diag_ends, metric, keep, matrices, two_inner, dots],
        pair + [ends_shape] * 2 + [sems((2,))], far_out=(0,),
    )
    all_dots = lax.all_to_all(all_dots, ("dom", "batch"), 0, 0)
    two_dom, two_corners = dom_swaps(*two_faces)
    two_batch = swaps(
        *ends_call((two_end, *two_corners, 0), (heat_end, *source_dom, 1)),
        "batch",
    )
    chunks = points // CHUNK
    head_next, defect, end_values, end_factors = call(
        last_kernel, "last", [block_shape] * 2 + [(2, points) + plane] * 2,
        [two_inner, two_ends, *two_dom, diag_inner, diag_ends, keep, all_dots,
         head_inner, head_ends, direction_inner, direction_ends, scaled_inner, scaled_ends],
        [block_shape, (3, 2) + ends_shape, block_shape, block_shape,
         sems((chunks, 6)), sems((chunks, 2))],
        far_in=range(8, 14), far_out=(0, 1),
    )
    defect, heat_next = call(
        close_kernel, "close", [block_shape] * 2,
        [defect, heat_next, *two_batch, end_values, end_factors, heat_values, heat_factors],
        [(2, 2, points) + plane, sems((2, 2))],
        far_in=(0, 1), far_out=(0, 1), aliases={0: 0, 1: 1},
    )
    shape = heat_state_element.shape
    return heat_next.reshape(shape), head_next.reshape(shape), defect.reshape(shape)


def solution(mesh):
    field = P("dom", None, "batch", None, None, None)
    triple = P(None, "dom", None, "batch", None, None, None)
    return jax.shard_map(
        shards,
        mesh=mesh,
        in_specs=(
            field, triple, triple, triple, field, field, field, P("dom", None, "batch", None),
        ),
        out_specs=(field, field, field),
        check_vma=False,
    )
```

```python
import functools
import math

import jax
import jax.numpy as jnp
import numpy as np
from jax import lax
from jax.experimental import pallas as pl
from jax.experimental.pallas import tpu as pltpu
from jax.sharding import PartitionSpec as P

QUAD_POINT_TALLY = 8
ROWS = QUAD_POINT_TALLY * QUAD_POINT_TALLY
LAST = ROWS - QUAD_POINT_TALLY
ITERS = 2

transport_increment = 0.02
conduction_increment = 0.002
step_dt = 0.02

VMEM_LIMIT = 12 * 1024 * 1024


def legendre_pair(order, point):
    before, current = (1.0, point)
    for level in range(2, order + 1):
        before, current = (
            current,
            ((2 * level - 1) * point * current - (level - 1) * before) / level,
        )
    return (current, before)


def tables():
    degree = QUAD_POINT_TALLY - 1
    points = [math.cos(math.pi * index / degree) for index in range(QUAD_POINT_TALLY)]
    for sweep in range(60):
        updated = []
        for point in points:
            top_value, below_value = legendre_pair(degree, point)
            updated.append(
                point - (point * top_value - below_value) / (QUAD_POINT_TALLY * top_value)
            )
        points = updated
    nodes = points[::-1]
    values = [legendre_pair(degree, point)[0] for point in nodes]
    weights = [2.0 / (degree * QUAD_POINT_TALLY * value * value) for value in values]
    deriv = np.zeros((QUAD_POINT_TALLY, QUAD_POINT_TALLY))
    for row in range(QUAD_POINT_TALLY):
        for col in range(QUAD_POINT_TALLY):
            if row != col:
                deriv[row, col] = values[row] / values[col] / (nodes[row] - nodes[col])
    corner_value = degree * QUAD_POINT_TALLY / 4.0
    deriv[0, 0] = -corner_value
    deriv[degree, degree] = corner_value
    return deriv, np.array(weights)


DERIV, WEIGHTS = tables()
HALF = QUAD_POINT_TALLY // 2


def line_tables(matrix):
    flipped = matrix[:, ::-1]
    even = (matrix + flipped)[:HALF, :HALF] / 2
    odd = (matrix - flipped)[:HALF, :HALF] / 2
    return even, odd


def deriv_line(matrix, values):
    even, odd = line_tables(matrix)
    plus = [values[l] + values[7 - l] for l in range(HALF)]
    minus = [values[l] - values[7 - l] for l in range(HALF)]
    result = [None] * QUAD_POINT_TALLY
    for i in range(HALF):
        from_plus = sum(float(even[i, l]) * plus[l] for l in range(HALF))
        from_minus = sum(float(odd[i, l]) * minus[l] for l in range(HALF))
        result[i] = from_minus + from_plus
        result[7 - i] = from_minus - from_plus
    return result


def square_line(matrix, values):
    even, odd = line_tables(matrix)
    plus = [values[l] + values[7 - l] for l in range(HALF)]
    minus = [values[l] - values[7 - l] for l in range(HALF)]
    result = [None] * QUAD_POINT_TALLY
    for i in range(HALF):
        from_plus = sum(float(even[i, l]) * plus[l] for l in range(HALF))
        from_minus = sum(float(odd[i, l]) * minus[l] for l in range(HALF))
        result[i] = from_plus + from_minus
        result[7 - i] = from_plus - from_minus
    return result


def stacked_matrix(matrix):
    whole = matrix.astype(np.float32)
    high = whole.astype(jnp.bfloat16)
    low = (whole - high.astype(np.float32)).astype(jnp.bfloat16)
    return np.concatenate([high, low, high], axis=1)


def height_product(stacked, values):
    high = values.astype(jnp.bfloat16)
    low = (values - high.astype(jnp.float32)).astype(jnp.bfloat16)
    both = jnp.concatenate([high, high, low], axis=0)
    return jnp.dot(stacked, both, preferred_element_type=jnp.float32)


def rows_of(j):
    return slice(QUAD_POINT_TALLY * j, QUAD_POINT_TALLY * (j + 1))


def height_weights(shape):
    level = lax.broadcasted_iota(jnp.int32, shape, 0)
    result = jnp.full(shape, float(WEIGHTS[0]), jnp.float32)
    for k in range(1, QUAD_POINT_TALLY):
        result = jnp.where(level == k, float(WEIGHTS[k]), result)
    return result


def copy_weights(shape):
    level = lax.broadcasted_iota(jnp.int32, shape, 0)
    layer = lax.broadcasted_iota(jnp.int32, shape, 1)
    shared = ((level == 0) & (layer > 0)) | (
        (level == QUAD_POINT_TALLY - 1) & (layer < shape[1] - 1)
    )
    return jnp.where(shared, 0.5, 1.0)


def side_weight(i, j):
    return (0.5 if i in (0, 7) else 1.0) * (0.5 if j in (0, 7) else 1.0)


HEIGHT, SIDE, HEIGHT_BACK, HEIGHT_SQUARE = (slice(n * ROWS, (n + 1) * ROWS) for n in range(4))
BOTH = slice(0, 2 * ROWS)


def constants():
    one = np.eye(QUAD_POINT_TALLY)
    return jnp.asarray(
        np.concatenate([
            stacked_matrix(np.kron(one, DERIV)),
            stacked_matrix(np.kron(DERIV, one)),
            stacked_matrix(np.kron(one, DERIV.T)),
            stacked_matrix(np.kron(one, (DERIV * DERIV).T)),
        ])
    )


def dom_sides():
    odd = lax.rem(lax.axis_index("dom"), 2)
    return 7 * (1 - odd), 7 * odd


def batch_sides():
    odd = lax.rem(lax.axis_index("batch"), 2)
    return 1 - odd, odd


UPPER = pl.ds(QUAD_POINT_TALLY - 1, QUAD_POINT_TALLY, stride=QUAD_POINT_TALLY)
LOWER = pl.ds(0, QUAD_POINT_TALLY, stride=QUAD_POINT_TALLY)
TAIL = slice(LAST, ROWS)
HEAD = slice(0, QUAD_POINT_TALLY)


def sum_heights(field, slot):
    layers = field.shape[3]
    lane = lax.broadcasted_iota(jnp.int32, (QUAD_POINT_TALLY, layers), 1)
    for i in range(field.shape[0]):
        upper = field[i, slot, UPPER, :]
        lower = field[i, slot, LOWER, :]
        above = jnp.where(lane < layers - 1, pltpu.roll(lower, layers - 1, 1), 0.0)
        below = jnp.where(lane > 0, pltpu.roll(upper, 1, 1), 0.0)
        field[i, slot, UPPER, :] = upper + above
        field[i, slot, LOWER, :] = lower + below


def face_rows(b):
    return slice(b * LAST, b * LAST + ROWS)


class Parts:
    def __init__(self, inner, ends):
        self.inner, self.ends = inner, ends
        self.blocks = inner.shape[1] + 2

    def at(self, b):
        if b in (0, self.blocks - 1):
            return self.ends, min(b, 1)
        return self.inner, b - 1

    def load(self, i, b, rows):
        field, slot = self.at(b)
        return field[i, slot, rows, :]


class Whole:
    def __init__(self, field):
        self.field, self.blocks = field, field.shape[1]

    def load(self, i, b, rows):
        return self.field[i, b, rows, :]


def joined(parts, i, b, out):
    out[...] = parts.load(i, b, slice(0, ROWS))
    if b > 0:
        out[HEAD, :] = out[HEAD, :] + parts.load(i, b - 1, TAIL)
    if b < parts.blocks - 1:
        out[TAIL, :] = out[TAIL, :] + parts.load(i, b + 1, HEAD)


def emit_faces(parts, first, second, corner=None, n=0):
    for side, face in zip(dom_sides(), (first, second)):
        for b in range(parts.blocks):
            joined(parts, side, b, face.at[n, face_rows(b)])
    if corner is not None:
        _, side = dom_sides()
        corner[n, rows_of(0), :] = parts.load(side, 0, HEAD)
        corner[n, rows_of(1), :] = parts.load(side, parts.blocks - 1, TAIL)


def emit_ends(parts, ends):
    for i in range(QUAD_POINT_TALLY):
        ends[0, i] = parts.load(i, 0, HEAD)
        ends[1, i] = parts.load(i, parts.blocks - 1, TAIL)


def assemble(parts, b, out, slot, dom_received, batch_received):
    for i in range(QUAD_POINT_TALLY):
        joined(parts, i, b, out.at[i, slot])
    for side, received in zip(dom_sides(), dom_received):
        out[side, slot] = out[side, slot] + received[face_rows(b), :]
    if batch_received is not None and b in (0, parts.blocks - 1):
        rows = HEAD if b == 0 else TAIL
        low, _ = batch_sides()
        from_first = low == (0 if b == 0 else 1)
        for i in range(QUAD_POINT_TALLY):
            received = jnp.where(from_first, batch_received[0][i], batch_received[1][i])
            out[i, slot, rows, :] = out[i, slot, rows, :] + received


def clear_top(field, slot, keep, b):
    for i in range(QUAD_POINT_TALLY):
        field[i, slot, UPPER, :] = field[i, slot, UPPER, :] * keep[i, b]


def apply_block(field, slot, metric, b, scratch_s, scratch_t, out, matrices, scale=1.0, extra=None):
    both, height_back = matrices[BOTH], matrices[HEIGHT_BACK]
    back = DERIV.T
    for i in range(QUAD_POINT_TALLY):
        slopes = height_product(both, field[i, slot])
        scratch_t[i] = slopes[:ROWS]
        scratch_s[i] = slopes[ROWS:]
    for j in range(QUAD_POINT_TALLY):
        rows = rows_of(j)
        along_r = deriv_line(DERIV, [field[i, slot, rows, :] for i in range(QUAD_POINT_TALLY)])
        flux_r = []
        additions = []
        for i in range(QUAD_POINT_TALLY):
            along_s, along_t = scratch_s[i, rows, :], scratch_t[i, rows, :]
            rr, ss, tt = (metric[n, i, b, rows, :] for n in range(3))
            rs, rt, st = (metric[n, i, b, rows, :] for n in range(3, 6))
            flux_r.append(rr * along_r[i] + rs * along_s + rt * along_t)
            scratch_s[i, rows, :] = rs * along_r[i] + ss * along_s + st * along_t
            scratch_t[i, rows, :] = rt * along_r[i] + st * along_s + tt * along_t
            if extra is not None:
                additions.append(extra(i, j, along_r[i], along_s, along_t))
        result = deriv_line(scale * back, flux_r)
        for i in range(QUAD_POINT_TALLY):
            out[i, slot, rows, :] = result[i] if extra is None else result[i] + additions[i]
    total = None
    for i in range(QUAD_POINT_TALLY):
        block = scratch_s[i]
        from_s = deriv_line(scale * back, [block[rows_of(j)] for j in range(QUAD_POINT_TALLY)])
        from_t = height_product(height_back, scratch_t[i])
        for j in range(QUAD_POINT_TALLY):
            rows = rows_of(j)
            term = from_t[rows] if scale == 1.0 else scale * from_t[rows]
            value = out[i, slot, rows, :] + from_s[j] + term
            out[i, slot, rows, :] = value
            if extra is None:
                term = field[i, slot, rows, :] * value
                total = term if total is None else total + term
    return total


def dot_weighted(left, right, slot):
    layers = left.shape[3]
    sums = {}
    for i in range(QUAD_POINT_TALLY):
        for j in range(QUAD_POINT_TALLY):
            weight = side_weight(i, j)
            term = left[i, slot, rows_of(j), :] * right[i, slot, rows_of(j), :]
            sums[weight] = sums[weight] + term if weight in sums else term
    total = sums[1.0] + 0.5 * sums[0.5] + 0.25 * sums[0.25]
    return total * copy_weights((QUAD_POINT_TALLY, layers))


def mass_faces_kernel(
    determinant, prior, first, second, ends, prior_ends, sides, planes, det_face, det_end, prior_face, prior_end,
    mass_face, mass_end, sems,
):
    blocks, layers = determinant.shape[1], first.shape[2]
    last = blocks - 1
    copies = []
    for n, i in enumerate((0, 7)):
        copies.append((determinant.at[i], det_face.at[n]))
        copies.append((prior.at[i], prior_face.at[n]))
    for n, (b, j) in enumerate(((0, 0), (last, 7))):
        copies.append((determinant.at[:, b, j], det_end.at[n]))
        copies.append((prior.at[:, b, j], prior_end.at[n]))
    started = [
        pltpu.make_async_copy(source, target, sems.at[n])
        for n, (source, target) in enumerate(copies)
    ]
    for copy in started:
        copy.start()
    for copy in started:
        copy.wait()
    weights = height_weights((QUAD_POINT_TALLY, layers))
    tile = (QUAD_POINT_TALLY, layers)
    for n, (end, plane) in enumerate(zip(batch_sides(), dom_sides())):
        sides[n] = jnp.full(tile, end.astype(jnp.float32))
        for i in range(QUAD_POINT_TALLY):
            planes[n, i] = jnp.full(tile, (plane == i).astype(jnp.float32))
    for n, i in enumerate((0, 7)):
        for b in range(blocks):
            for j in range(QUAD_POINT_TALLY):
                weight = weights * float(WEIGHTS[i] * WEIGHTS[j])
                value = weight * det_face[n, b, j].astype(jnp.float32)
                mass_face[0, n, b, rows_of(j), :] = value
                mass_face[1, n, b, rows_of(j), :] = value * prior_face[n, b, j]
    for side, j in enumerate((0, 7)):
        for i in range(QUAD_POINT_TALLY):
            weight = weights * float(WEIGHTS[i] * WEIGHTS[j])
            value = weight * det_end[side, i].astype(jnp.float32)
            mass_end[0, 0, side, rows_of(i), :] = value
            mass_end[1, 0, side, rows_of(i), :] = value * prior_end[side, i]
    for n in range(2):
        for b in range(blocks):
            sum_heights(mass_face.at[n], b)
        for side in range(2):
            sum_heights(mass_end.at[n], side)
            for i in range(QUAD_POINT_TALLY):
                (ends, prior_ends)[n][0, side, i] = mass_end[n, 0, side, rows_of(i), :]
        for b in range(blocks - 1):
            for face in range(2):
                total = mass_face[n, face, b, TAIL, :] + mass_face[n, face, b + 1, HEAD, :]
                mass_face[n, face, b, TAIL, :] = total
                mass_face[n, face, b + 1, HEAD, :] = total
        odd, _ = dom_sides()
        face_first = jnp.minimum(odd, 1)
        for b in range(blocks):
            first[n, face_rows(b), :] = mass_face[n, face_first, b]
            second[n, face_rows(b), :] = mass_face[n, 1 - face_first, b]


def prepare_kernel(
    determinant, prior, pure, mixed, matrices, mass, mass_prior, metric, diagonal,
    det_in, prior_in, pure_in, mixed_in, sems,
):
    blocks, layers = diagonal.shape[1], diagonal.shape[3]
    weights = height_weights((QUAD_POINT_TALLY, layers))
    level = lax.broadcasted_iota(jnp.int32, (QUAD_POINT_TALLY, layers), 0)
    ends = [float(DERIV[i, i]) for i in range(QUAD_POINT_TALLY)]
    height_ends = jnp.where(level == 0, ends[0], jnp.where(level == 7, ends[7], 0.0))
    squares = DERIV * DERIV

    def mass_copies(b):
        return (
            pltpu.make_async_copy(determinant.at[:, b], det_in.at[:, b], sems.at[0, b]),
            pltpu.make_async_copy(prior.at[:, b], prior_in.at[:, b], sems.at[1, b]),
        )

    def metric_copies(b):
        return (
            pltpu.make_async_copy(pure.at[:, :, b], pure_in.at[:, :, b], sems.at[2, b]),
            pltpu.make_async_copy(mixed.at[:, :, b], mixed_in.at[:, :, b], sems.at[3, b]),
        )

    for copies in (mass_copies, metric_copies):
        for b in range(blocks):
            for copy in copies(b):
                copy.start()

    def mass_block(b, carry):
        for copy in mass_copies(b):
            copy.wait()
        for i in range(QUAD_POINT_TALLY):
            for j in range(QUAD_POINT_TALLY):
                weight = weights * float(WEIGHTS[i] * WEIGHTS[j])
                value = weight * det_in[i, b, j].astype(jnp.float32)
                mass[i, b, rows_of(j), :] = value
                mass_prior[i, b, rows_of(j), :] = value * prior_in[i, b, j]
        sum_heights(mass, b)
        sum_heights(mass_prior, b)
        return carry

    def metric_block(b, carry):
        for copy in metric_copies(b):
            copy.wait()
        for i in range(QUAD_POINT_TALLY):
            for j in range(QUAD_POINT_TALLY):
                weight = weights * float(WEIGHTS[i] * WEIGHTS[j])
                for n in range(3):
                    metric[n, i, b, rows_of(j), :] = weight * pure_in[n, i, b, j].astype(
                        jnp.float32
                    )
                    metric[n + 3, i, b, rows_of(j), :] = weight * mixed_in[n, i, b, j].astype(
                        jnp.float32
                    )
        for j in range(QUAD_POINT_TALLY):
            line = square_line(
                squares.T, [metric[0, i, b, rows_of(j), :] for i in range(QUAD_POINT_TALLY)]
            )
            for i in range(QUAD_POINT_TALLY):
                diagonal[i, b, rows_of(j), :] = line[i]
        for i in range(QUAD_POINT_TALLY):
            line = square_line(
                squares.T, [metric[1, i, b, rows_of(j), :] for j in range(QUAD_POINT_TALLY)]
            )
            from_t = height_product(matrices[HEIGHT_SQUARE], metric[2, i, b])
            for j in range(QUAD_POINT_TALLY):
                rows = rows_of(j)
                value = diagonal[i, b, rows, :] + line[j] + from_t[rows]
                if ends[i] != 0.0 and ends[j] != 0.0:
                    value = value + (2.0 * ends[i] * ends[j]) * metric[3, i, b, rows, :]
                if ends[i] != 0.0:
                    value = value + (2.0 * ends[i]) * height_ends * metric[4, i, b, rows, :]
                if ends[j] != 0.0:
                    value = value + (2.0 * ends[j]) * height_ends * metric[5, i, b, rows, :]
                diagonal[i, b, rows, :] = value
        sum_heights(diagonal, b)
        return carry

    lax.fori_loop(0, blocks, mass_block, 0)
    lax.fori_loop(0, blocks, metric_block, 0)


def source_kernel(
    metric, heat, wind, determinant, diagonal, matrices,
    numerator, first, second, diag_ends, heat_ends, scratch_s, scratch_t,
):
    blocks, layers = numerator.shape[1], numerator.shape[3]
    weights = height_weights((QUAD_POINT_TALLY, layers))

    def block(b, carry):
        def extra(i, j, along_r, along_s, along_t):
            weight = weights * float(WEIGHTS[i] * WEIGHTS[j])
            convection = (
                wind[0, i, b, j].astype(jnp.float32) * along_r
                + wind[1, i, b, j].astype(jnp.float32) * along_s
                + wind[2, i, b, j].astype(jnp.float32) * along_t
            )
            return weight * (
                determinant[i, b, j].astype(jnp.float32) * heat[i, b, rows_of(j), :]
                - transport_increment * convection
            )

        apply_block(
            heat, b, metric, b, scratch_s, scratch_t, numerator, matrices,
            -conduction_increment, extra,
        )
        sum_heights(numerator, b)
        return carry

    lax.fori_loop(0, blocks, block, 0)
    for n, (field, ends) in enumerate(((diagonal, diag_ends), (numerator, heat_ends))):
        emit_faces(Whole(field), first, second, n=n)
        emit_ends(Whole(field), ends.at[0])


def ends_kernel(offsets, *refs):
    inputs, (first, second) = refs[: 3 * len(offsets)], refs[3 * len(offsets) :]
    for n, offset in enumerate(offsets):
        ends, *received = inputs[3 * n : 3 * n + 3]
        lasts = [face.shape[1] - QUAD_POINT_TALLY for face in received]
        for side, target in zip(batch_sides(), (first, second)):
            for i in range(QUAD_POINT_TALLY):
                target[n, i] = ends[0, side, i]
            for dom_side, face, last in zip(dom_sides(), received, lasts):
                rows = pl.ds(pl.multiple_of(side * last, QUAD_POINT_TALLY), QUAD_POINT_TALLY)
                target[n, dom_side] = target[n, dom_side] + face[offset, rows, :]


def elements(inner, blocks):
    return list(enumerate(range(1, blocks - 1) if inner else (0, blocks - 1)))


class Sending:
    def __init__(self, sems):
        self.sems, self.copies = sems, []

    def start(self, source, target):
        copy = pltpu.make_async_copy(source, target, self.sems.at[len(self.copies)])
        copy.start()
        self.copies.append(copy)

    def wait(self):
        for copy in self.copies:
            copy.wait()


def start_source(determinant, spread, b):
    layers = spread.shape[3]
    weights = height_weights((QUAD_POINT_TALLY, layers))

    def extra(i, j, along_r, along_s, along_t):
        weight = weights * float(-WEIGHTS[i] * WEIGHTS[j] / step_dt)
        return (weight * determinant[i, b, j].astype(jnp.float32)) * spread[i, b, rows_of(j), :]

    return extra


def assemble_head(mass, mass_prior, dom, batch, keep, slot, b, mass_inverse, head):
    for n, (field, out) in enumerate(((mass, mass_inverse), (mass_prior, head))):
        assemble(
            Whole(field), b, out, slot, tuple(face.at[n] for face in dom),
            batch and tuple(face.at[n] for face in batch),
        )
    clear_top(head, slot, keep, b)
    for i in range(QUAD_POINT_TALLY):
        inverse = 1.0 / mass_inverse[i, slot]
        mass_inverse[i, slot] = inverse
        head[i, slot] = head[i, slot] * inverse


def start_inner_kernel(
    mass, mass_prior, dom_first, dom_second, metric, spread, determinant, keep, matrices,
    head_out, mass_inverse, residual, scratch_s, scratch_t, head, sems,
):
    blocks = mass.shape[1]
    sending = Sending(sems)
    for slot, b in elements(True, blocks):
        assemble_head(
            mass, mass_prior, (dom_first, dom_second), None, keep, slot, b, mass_inverse, head
        )
        sending.start(head.at[:, slot], head_out.at[:, slot])
    for slot, b in elements(True, blocks):
        apply_block(
            head, slot, metric, b, scratch_s, scratch_t, residual, matrices, -1.0,
            start_source(determinant, spread, b),
        )
        sum_heights(residual, slot)
    sending.wait()


def start_ends_kernel(
    mass, mass_prior, dom_first, dom_second, batch_first, batch_second,
    metric, spread, determinant, keep, matrices, residual_inner,
    head_out, mass_inverse, residual, first, second, corner, ends,
    scratch_s, scratch_t, head, sems,
):
    blocks = mass.shape[1]
    sending = Sending(sems)
    for slot, b in elements(False, blocks):
        assemble_head(
            mass, mass_prior, (dom_first, dom_second), (batch_first, batch_second), keep,
            slot, b, mass_inverse, head,
        )
        sending.start(head.at[:, slot], head_out.at[:, slot])
    for slot, b in elements(False, blocks):
        apply_block(
            head, slot, metric, b, scratch_s, scratch_t, residual, matrices, -1.0,
            start_source(determinant, spread, b),
        )
        sum_heights(residual, slot)
    parts = Parts(residual_inner, residual)
    emit_faces(parts, first, second, corner)
    emit_ends(parts, ends.at[0])
    sending.wait()


def row_sums(*parts):
    rows = [jnp.sum(part, axis=0, keepdims=True) for part in parts]
    rows.append(jnp.zeros((QUAD_POINT_TALLY - len(parts), parts[0].shape[1]), jnp.float32))
    return jnp.concatenate(rows, axis=0)


def assemble_direction(
    residual_parts, diagonal, res_dom, diag_dom, batch, keep, slot, b,
    residual, diag_inverse, direction,
):
    assemble(
        residual_parts, b, residual, slot, tuple(face.at[0] for face in res_dom),
        batch and tuple(face.at[0] for face in batch),
    )
    assemble(
        Whole(diagonal), b, diag_inverse, slot, tuple(face.at[0] for face in diag_dom),
        batch and tuple(face.at[1] for face in batch),
    )
    clear_top(residual, slot, keep, b)
    for i in range(QUAD_POINT_TALLY):
        inverse = 1.0 / diag_inverse[i, slot]
        diag_inverse[i, slot] = inverse
        direction[i, slot] = residual[i, slot] * inverse


def apply_dots(left, field, inner, metric, scratch_s, scratch_t, out, matrices):
    energy = product = 0.0
    for slot, b in elements(inner, metric.shape[2]):
        energy += apply_block(field, slot, metric, b, scratch_s, scratch_t, out, matrices)
        product += dot_weighted(left, field, slot)
        sum_heights(out, slot)
    return product, energy


def first_inner_kernel(
    residual_inner, residual_ends, diagonal, res_first, res_second, diag_first, diag_second,
    metric, keep, matrices,
    direction_out, diag_inverse, image, dots, scratch_s, scratch_t, residual, direction, sems,
):
    sending = Sending(sems)
    for slot, b in elements(True, diagonal.shape[1]):
        assemble_direction(
            Parts(residual_inner, residual_ends), diagonal, (res_first, res_second),
            (diag_first, diag_second), None, keep, slot, b, residual, diag_inverse, direction,
        )
        sending.start(direction.at[:, slot], direction_out.at[:, slot])
    dots[...] = row_sums(
        *apply_dots(residual, direction, True, metric, scratch_s, scratch_t, image, matrices)
    )
    sending.wait()


def first_ends_kernel(
    residual_inner, residual_ends, diagonal, res_first, res_second, diag_first, diag_second,
    batch_first, batch_second, metric, keep, matrices, image_inner, dots_inner,
    direction_out, diag_inverse, image, first, second, corner, ends, dots,
    scratch_s, scratch_t, residual, direction, sems,
):
    sending = Sending(sems)
    for slot, b in elements(False, diagonal.shape[1]):
        assemble_direction(
            Parts(residual_inner, residual_ends), diagonal, (res_first, res_second),
            (diag_first, diag_second), (batch_first, batch_second), keep, slot, b,
            residual, diag_inverse, direction,
        )
        sending.start(direction.at[:, slot], direction_out.at[:, slot])
    dots[...] = dots_inner[...] + row_sums(
        *apply_dots(residual, direction, False, metric, scratch_s, scratch_t, image, matrices)
    )
    parts = Parts(image_inner, image)
    emit_faces(parts, first, second, corner)
    emit_ends(parts, ends.at[0])
    sending.wait()


def second_inner_kernel(
    image_inner, image_ends, dom_first, dom_second, diag_inverse, metric, keep, matrices, dots_in,
    scaled_out, image_two, dots, scratch_s, scratch_t, image, scaled, sems,
):
    parts = Parts(image_inner, image_ends)
    sending = Sending(sems)
    for slot, b in elements(True, parts.blocks):
        assemble(parts, b, image, slot, (dom_first.at[0], dom_second.at[0]), None)
        clear_top(image, slot, keep, b)
        for i in range(QUAD_POINT_TALLY):
            scaled[i, slot] = image[i, slot] * diag_inverse[i, slot]
        sending.start(scaled.at[:, slot], scaled_out.at[:, slot])
    product, energy = apply_dots(
        image, scaled, True, metric, scratch_s, scratch_t, image_two, matrices
    )
    nothing = jnp.zeros_like(energy)
    dots[...] = dots_in[...] + row_sums(nothing, nothing, product, energy)
    sending.wait()


def second_ends_kernel(
    image_inner, image_ends, dom_first, dom_second, batch_first, batch_second,
    diag_inverse, metric, keep, matrices, two_inner, dots_in,
    scaled_out, image_two, first, second, corner, ends, all_dots,
    scratch_s, scratch_t, image, scaled, dots_out, sems,
):
    parts = Parts(image_inner, image_ends)
    sending = Sending(sems)
    for slot, b in elements(False, parts.blocks):
        assemble(
            parts, b, image, slot, (dom_first.at[0], dom_second.at[0]),
            (batch_first.at[0], batch_second.at[0]),
        )
        clear_top(image, slot, keep, b)
        for i in range(QUAD_POINT_TALLY):
            scaled[i, slot] = image[i, slot] * diag_inverse[i, slot]
        sending.start(scaled.at[:, slot], scaled_out.at[:, slot])
    product, energy = apply_dots(
        image, scaled, False, metric, scratch_s, scratch_t, image_two, matrices
    )
    nothing = jnp.zeros_like(energy)
    sums = dots_in[...] + row_sums(nothing, nothing, product, energy)
    for n in range(all_dots.shape[0]):
        dots_out[n] = sums
    sending.start(dots_out, all_dots)
    parts = Parts(two_inner, image_two)
    emit_faces(parts, first, second, corner)
    emit_ends(parts, ends.at[0])
    sending.wait()


def heat_kernel(
    numerator, dom_first, dom_second, inverse_inner, inverse_ends, heat, values, factors
):
    blocks = heat.shape[1]
    inverse = Parts(inverse_inner, inverse_ends)
    for b in range(blocks):
        assemble(Whole(numerator), b, heat, b, (dom_first.at[1], dom_second.at[1]), None)
        for i in range(QUAD_POINT_TALLY):
            heat[i, b] = heat[i, b] * inverse.load(i, b, slice(0, ROWS))
    for side, (b, rows) in enumerate(((0, HEAD), (blocks - 1, TAIL))):
        for i in range(QUAD_POINT_TALLY):
            values[side, i] = heat[i, b, rows, :]
            factors[side, i] = inverse.load(i, b, rows)


CHUNK = 1


def last_kernel(
    image_inner, image_ends, dom_first, dom_second, diag_inner, diag_ends, keep, all_dots,
    head_inner, head_ends, direction_inner, direction_ends, scaled_inner, scaled_ends,
    out_head, out_defect, end_values, end_factors,
    image, far, result_head, result_defect, sems_in, sems_out,
):
    sources = (
        head_inner, head_ends, direction_inner, direction_ends, scaled_inner, scaled_ends
    )
    chunks = QUAD_POINT_TALLY // CHUNK
    arriving = []
    for c in range(chunks):
        planes = pl.ds(c * CHUNK, CHUNK)
        arriving.append([
            pltpu.make_async_copy(
                source.at[planes], far.at[n // 2, n % 2, planes], sems_in.at[c, n]
            )
            for n, source in enumerate(sources)
        ])
        for copy in arriving[-1]:
            copy.start()
    parts, inverses = Parts(image_inner, image_ends), Parts(diag_inner, diag_ends)
    blocks, layers = parts.blocks, image.shape[3]
    level = lax.broadcasted_iota(jnp.int32, (QUAD_POINT_TALLY, layers), 0)
    sums = all_dots[0]
    for n in range(1, all_dots.shape[0]):
        sums = sums + all_dots[n]
    sums = jnp.sum(sums, axis=1, keepdims=True)
    inner, energy, cross, energy_two = (sums[n : n + 1] for n in range(4))
    step = inner / energy
    following = step * step * cross - inner
    growth = 1.0 + following / inner
    curvature = growth * growth * energy - 2.0 * growth * step * cross + step * step * energy_two
    step_two = following / curvature
    along_direction = step + step_two * growth
    along_scaled = step * step_two
    whole = slice(0, ROWS)
    for b in range(blocks):
        for i in range(QUAD_POINT_TALLY):
            joined(parts, i, b, image.at[i, b])
        for side, received in zip(dom_sides(), (dom_first, dom_second)):
            image[side, b] = image[side, b] + received[0, face_rows(b), :]
        clear_top(image, b, keep, b)
    leaving = []
    for c in range(chunks):
        planes = pl.ds(c * CHUNK, CHUNK)
        for copy in arriving[c]:
            copy.wait()
        for i in range(c * CHUNK, (c + 1) * CHUNK):
            for b in range(blocks):
                kind, slot = (1, min(b, 1)) if b in (0, blocks - 1) else (0, b - 1)
                start, change = far[1, kind, i, slot], far[2, kind, i, slot]
                inverse = inverses.load(i, b, whole)
                result_head[i, b] = (
                    far[0, kind, i, slot] + along_direction * start - along_scaled * change
                )
                result_defect[i, b] = (
                    start - along_direction * change + along_scaled * (image[i, b] * inverse)
                )
            for side, (b, j) in enumerate(((0, 0), (blocks - 1, 7))):
                end_values[side, i] = result_defect[i, b, rows_of(j), :]
                top = jnp.where(level == 7, keep[i, b, j : j + 1, :], 1.0)
                end_factors[side, i] = along_scaled * top * inverses.load(i, b, rows_of(j))
        for n, (source, target) in enumerate(
            ((result_head, out_head), (result_defect, out_defect))
        ):
            copy = pltpu.make_async_copy(source.at[planes], target.at[planes], sems_out.at[c, n])
            copy.start()
            leaving.append(copy)
    for copy in leaving:
        copy.wait()


def close_kernel(
    defect, heat, batch_first, batch_second, defect_values, defect_factors, heat_values,
    heat_factors, out_defect, out_heat, rows, sems,
):
    del defect, heat
    low, _ = batch_sides()
    copies = []
    for n, (values, factors, out) in enumerate((
        (defect_values, defect_factors, out_defect), (heat_values, heat_factors, out_heat)
    )):
        for side, (b, start) in enumerate(((0, 0), (out.shape[1] - 1, LAST))):
            for i in range(QUAD_POINT_TALLY):
                received = jnp.where(low == side, batch_first[n, i], batch_second[n, i])
                rows[n, side, i] = values[side, i] + factors[side, i] * received
            copy = pltpu.make_async_copy(
                rows.at[n, side], out.at[:, b, pl.ds(start, QUAD_POINT_TALLY), :],
                sems.at[n, side],
            )
            copy.start()
            copies.append(copy)
    for copy in copies:
        copy.wait()


COST = {
    "mass_faces": 2, "prepare": 10, "source": 14, "start_inner": 8, "start_faces": 4,
    "start_ends": 8, "first_inner": 8, "first_faces": 4, "first_ends": 6, "heat": 4,
    "second_inner": 8, "second_ends": 8, "last": 12, "close": 2,
}


def call(kernel, name, outs, args, scratch=(), far_in=(), far_out=(), aliases=None):
    near, far = pl.BlockSpec(memory_space=pltpu.VMEM), pl.BlockSpec(memory_space=pltpu.HBM)
    args = [
        pltpu.with_memory_space_constraint(arg, pltpu.HBM) if n in far_in else arg
        for n, arg in enumerate(args)
    ]
    return pl.pallas_call(
        kernel,
        name=name,
        out_shape=[
            (pltpu.HBM if n in far_out else jax.ShapeDtypeStruct)(shape, jnp.float32)
            for n, shape in enumerate(outs)
        ],
        in_specs=[far if n in far_in else near for n in range(len(args))],
        out_specs=[far if n in far_out else near for n in range(len(outs))],
        scratch_shapes=[
            shape if not isinstance(shape, tuple) else pltpu.VMEM(shape, jnp.float32)
            for shape in scratch
        ],
        input_output_aliases=aliases or {},
        cost_estimate=pl.CostEstimate(
            flops=0, bytes_accessed=COST.get(name, 0) * 1000000, transcendentals=0
        ),
        compiler_params=pltpu.CompilerParams(vmem_limit_bytes=VMEM_LIMIT),
    )(*args)


def near_swap(array, axis):
    count = lax.axis_size(axis)
    return lax.ppermute(array, axis, [(index, index ^ 1) for index in range(count)])


def far_swap(array, axis):
    count = lax.axis_size(axis)
    pairs = [(index, (((index + 1) ^ 1) - 1) % count) for index in range(count)]
    return lax.ppermute(array, axis, pairs)


def swaps(first, second, axis):
    return near_swap(first, axis), far_swap(second, axis)


def shards(
    heat_state_element,
    wind_reference_flux,
    geometric_pure_factors,
    geometric_mixed_factors,
    mapping_determinant,
    velocity_source_spread,
    prior_head_state,
    exit_boundary_marks,
):
    _, points, blocks, _, _, layers = heat_state_element.shape
    block_shape = (points, blocks, ROWS, layers)
    inner_shape = (points, blocks - 2, ROWS, layers)
    ends_shape = (points, 2, ROWS, layers)
    heat = heat_state_element.reshape(block_shape)
    spread = velocity_source_spread.reshape(block_shape)
    prior = prior_head_state[0]
    wind, pure, mixed = (
        array.reshape(array.shape[:1] + array.shape[2:])
        for array in (wind_reference_flux, geometric_pure_factors, geometric_mixed_factors)
    )
    determinant = mapping_determinant[0]
    layer = lax.broadcasted_iota(jnp.int32, (points, blocks, points, layers), 3)
    marks = exit_boundary_marks[0].astype(jnp.float32)[:, :, :, None]
    keep = jnp.where(layer == layers - 1, 1.0 - marks, 1.0)
    matrices = constants()

    end_shape = (1, 2, points, points, layers)

    def faces(count):
        face = (count, blocks * LAST + QUAD_POINT_TALLY, layers)
        return [face] * 2

    corner_shape = (1, 2 * QUAD_POINT_TALLY, layers)

    def dom_swaps(first, second, corner):
        corner = far_swap(corner, "dom")
        near = near_swap(first, "dom")
        return (near, far_swap(second, "dom")), (near, corner)

    def ends_call(*groups):
        results = []
        for side in range(2):
            high = sides[side] > 0.0
            fields = []
            for ends, *received, place in groups:
                field = jnp.where(high[None], ends[0, 1], ends[0, 0])
                for plane_mask, face in zip(planes, received):
                    tail = face[place, face.shape[1] - points :]
                    rows = jnp.where(high, tail, face[place, :points])
                    field = field + plane_mask * rows[None]
                fields.append(field)
            results.append(jnp.stack(fields))
        return results

    def mass_call(ends, *received):
        return call(
            functools.partial(ends_kernel, (0, 1)), "mass_ends",
            [(2, points, points, layers)] * 2, [ends[0], *received, ends[1], *received],
        )

    pair = [(points, ROWS, layers)] * 2
    plane = (points, layers)

    *mass_faces, mass_end, prior_end, sides, planes = call(
        mass_faces_kernel, "mass_faces",
        faces(2) + [end_shape] * 2 + [(2,) + plane, (2, points) + plane], [determinant, prior],
        [
            pltpu.VMEM((2, blocks, points, points, layers), jnp.bfloat16),
            pltpu.VMEM((2, points, points, layers), jnp.bfloat16),
            (2, blocks, points, points, layers),
            (2, points, points, layers),
            (2, 2, blocks, ROWS, layers),
            (2, 1, 2, ROWS, layers),
            pltpu.SemaphoreType.DMA((8,)),
        ],
        far_in=(0, 1),
    )
    mass_dom = swaps(*mass_faces, "dom")
    mass, mass_prior, metric, diagonal = call(
        prepare_kernel, "prepare", [block_shape] * 2 + [(6,) + block_shape, block_shape],
        [determinant, prior, pure, mixed, matrices],
        [
            pltpu.VMEM(determinant.shape, jnp.bfloat16),
            prior.shape,
            pltpu.VMEM(pure.shape, jnp.bfloat16),
            pltpu.VMEM(mixed.shape, jnp.bfloat16),
            pltpu.SemaphoreType.DMA((4, blocks)),
        ],
        far_in=range(4),
    )
    numerator, *source_faces, diag_end, heat_end = call(
        source_kernel, "source", [block_shape] + faces(2) + [end_shape] * 2,
        [metric, heat, wind, determinant, diagonal, matrices], pair,
    )
    source_dom = swaps(*source_faces, "dom")
    mass_batch = swaps(
        *mass_call((mass_end, prior_end), *mass_dom), "batch"
    )
    sems = pltpu.SemaphoreType.DMA
    common = [metric, spread, determinant]
    head_inner, inverse_inner, residual_inner = call(
        start_inner_kernel, "start_inner", [inner_shape] * 3,
        [mass, mass_prior, *mass_dom, *common, keep, matrices],
        pair + [inner_shape, sems((blocks,))], far_out=(0,),
    )
    head_ends, inverse_ends, residual_ends, *res_faces, res_end = call(
        start_ends_kernel, "start_ends", [ends_shape] * 3 + faces(1) + [corner_shape, end_shape],
        [mass, mass_prior, *mass_dom, *mass_batch, *common, keep, matrices, residual_inner],
        pair + [ends_shape, sems((2,))], far_out=(0,),
    )
    res_dom, res_corners = dom_swaps(*res_faces)
    res_batch = swaps(
        *ends_call((res_end, *res_corners, 0), (diag_end, *source_dom, 0)),
        "batch",
    )
    residual = [residual_inner, residual_ends, diagonal, *res_dom, *source_dom]
    direction_inner, diag_inner, image_inner, dots_inner = call(
        first_inner_kernel, "first_inner", [inner_shape] * 3 + [plane],
        [*residual, metric, keep, matrices], pair + [inner_shape] * 2 + [sems((blocks,))],
        far_out=(0,),
    )
    direction_ends, diag_ends, image_ends, *image_faces, image_end, dots = call(
        first_ends_kernel, "first_ends", [ends_shape] * 3 + faces(1) + [corner_shape, end_shape, plane],
        [*residual, *res_batch, metric, keep, matrices, image_inner, dots_inner],
        pair + [ends_shape] * 2 + [sems((2,))], far_out=(0,),
    )
    image_dom, image_corners = dom_swaps(*image_faces)
    heat_next, heat_values, heat_factors = call(
        heat_kernel, "heat", [block_shape] + [(2, points) + plane] * 2,
        [numerator, *source_dom, inverse_inner, inverse_ends],
    )
    image_batch = swaps(*ends_call((image_end, *image_corners, 0)), "batch")
    heat_next, received = lax.optimization_barrier((heat_next, image_batch[0]))
    image_batch = (received, image_batch[1])
    count = lax.axis_size("dom") * lax.axis_size("batch")
    image = [image_inner, image_ends, *image_dom]
    scaled_inner, two_inner, dots = call(
        second_inner_kernel, "second_inner", [inner_shape] * 2 + [plane],
        [*image, diag_inner, metric, keep, matrices, dots],
        pair + [inner_shape] * 2 + [sems((blocks,))], far_out=(0,),
    )
    scaled_ends, two_ends, *two_faces, two_end, all_dots = call(
        second_ends_kernel, "second_ends",
        [ends_shape] * 2 + faces(1) + [corner_shape, end_shape, (count,) + plane],
        [*image, *image_batch, diag_ends, metric, keep, matrices, two_inner, dots],
        pair + [ends_shape] * 2 + [(count,) + plane, sems((3,))], far_out=(0, 6),
    )
    all_dots = lax.all_to_all(all_dots, ("dom", "batch"), 0, 0)
    two_dom, two_corners = dom_swaps(*two_faces)
    two_batch = swaps(
        *ends_call((two_end, *two_corners, 0), (heat_end, *source_dom, 1)),
        "batch",
    )
    chunks = points // CHUNK
    head_next, defect, end_values, end_factors = call(
        last_kernel, "last", [block_shape] * 2 + [(2, points) + plane] * 2,
        [two_inner, two_ends, *two_dom, diag_inner, diag_ends, keep, all_dots,
         head_inner, head_ends, direction_inner, direction_ends, scaled_inner, scaled_ends],
        [block_shape, (3, 2) + ends_shape, block_shape, block_shape,
         sems((chunks, 6)), sems((chunks, 2))],
        far_in=range(8, 14), far_out=(0, 1),
    )
    defect, heat_next = call(
        close_kernel, "close", [block_shape] * 2,
        [defect, heat_next, *two_batch, end_values, end_factors, heat_values, heat_factors],
        [(2, 2, points) + plane, sems((2, 2))],
        far_in=(0, 1), far_out=(0, 1), aliases={0: 0, 1: 1},
    )
    shape = heat_state_element.shape
    return heat_next.reshape(shape), head_next.reshape(shape), defect.reshape(shape)


def solution(mesh):
    field = P("dom", None, "batch", None, None, None)
    triple = P(None, "dom", None, "batch", None, None, None)
    return jax.shard_map(
        shards,
        mesh=mesh,
        in_specs=(
            field, triple, triple, triple, field, field, field, P("dom", None, "batch", None),
        ),
        out_specs=(field, field, field),
        check_vma=False,
    )
```
